768 devices in a mesh: row: 16 (over y, z_hi), col: 12 (over z_lo, core), chan: 4 (over x).
Axes of the slice: x: 4, y: 8, z: 12 (z_hi: 2, z_lo: 6; z = z_hi * 6 + z_lo), core: 2. Of those that a mesh axis runs over, the one named last changes fastest.
Arguments:
- velocity: float32 [16, 3, 256, 3072], P('chan', None, 'row', 'col'), may hold values from -6 to 6
- lift_weight: float32 [32, 3], replicated, may hold values from -3.5 to 3.5
- lift_bias: float32 [32], replicated, may hold values from -3 to 3
- conv_weight: bfloat16 [27, 32, 32], P(None, 'chan'), may hold values from -0.21875 to 0.21875
- conv_bias: bfloat16 [32], P('chan'), may hold values from -3 to 3
- head_weight: bfloat16 [6, 32], P(None, 'chan'), may hold values from -1 to 1
Outputs:
- velocity_next: float32 [16, 3, 256, 3072], P('chan', None, 'row', 'col')
- stress: float32 [8, 6, 128, 1536], P('chan', None, 'row', 'col')
The draws below stay inside these ranges and needn't reach their ends.
All inputs are finite; a program needn't handle non-finite values.
Results may differ from the reference program's by a relative error of at most 0.0003.
Values may be sent and summed in bfloat16 or wider, within the bound.
A program may use at most 64 MiB of HBM per device.

```python
import jax
import jax.numpy as jnp
from jax import lax

HID = 32
NX = 16
NY = 256
NZ = 3072


def steps_of(key, extent, cuts, least, high):
    def one(position, blocks):
        draws = jax.random.uniform(jax.random.fold_in(jax.random.fold_in(key, 6), position), (blocks,), jnp.float32, least / len(cuts), high / len(cuts))
        return jnp.repeat(jnp.exp(draws), extent[position] // blocks).reshape((-1,) + (1,) * (len(extent) - position - 1))

    level = one(*cuts[0])
    for cut in cuts[1:]:
        level = level * one(*cut)
    return level


def scatter_about(stream_key, dims, scale, most, pieces=(), kind=jnp.bfloat16):
    result = scale * jax.random.normal(stream_key, dims, jnp.float32)
    if pieces:
        result = result * steps_of(stream_key, dims, pieces, -0.22, 0.18)
    return jnp.clip(result, -most, most).astype(kind)


def setup_inputs(seed: int = 0) -> dict:
    key_of = jax.random.split(jax.random.key(seed), 7)
    return {
        "velocity": scatter_about(key_of[0], (NX, 3, NY, NZ), 1.0, 6.0, ((0, 4), (2, 16), (3, 12)), jnp.float32),
        "lift_weight": scatter_about(key_of[1], (HID, 3), 3 ** -0.5, 3.5, (), jnp.float32),
        "lift_bias": scatter_about(key_of[2], (HID,), 0.5, 3.0, (), jnp.float32),
        "conv_weight": scatter_about(key_of[3], (27, HID, HID), (27 * HID) ** -0.5, 0.21875, ((1, 4),)),
        "conv_bias": scatter_about(key_of[4], (HID,), 0.5, 3.0, ((0, 4),)),
        "head_weight": scatter_about(key_of[5], (6, HID), HID ** -0.5, 1.0, ((1, 4),)),
    }


step_size = 0.1


def coarsen(velocity):
    nplanes, comps, ylen, zlen = velocity.shape
    blocks = velocity.reshape(nplanes // 2, 2, comps, ylen // 2, 2, zlen // 2, 2)
    return jnp.mean(blocks, axis=(1, 4, 6))


def lift(box, lift_weight, lift_bias):
    linear = jnp.einsum("ci,xiyz->xcyz", lift_weight, box, precision=lax.Precision.HIGHEST)
    return jnp.tanh(linear + lift_bias[None, :, None, None])


def upsample(field):
    return jnp.repeat(jnp.repeat(jnp.repeat(field, 2, 0), 2, 2), 2, 3)


def fluxes(velocity, fine):
    ux = velocity[:, 0]
    uy = velocity[:, 1]
    uz = velocity[:, 2]
    return jnp.stack([ux * ux + fine[:, 0], uy * uy + fine[:, 1], uz * uz + fine[:, 2],
                      ux * uy + fine[:, 3], ux * uz + fine[:, 4], uy * uz + fine[:, 5]], axis=1)


def derive(flux, axis):
    def moved(offset):
        return jnp.roll(flux, 3 - offset, axis)
    return (45.0 * (moved(4) - moved(2)) - 9.0 * (moved(5) - moved(1)) + (moved(6) - moved(0))) / 60.0


def reference(velocity, lift_weight, lift_bias, conv_weight, conv_bias, head_weight):
    box = coarsen(velocity)
    hidden = lift(box, lift_weight, lift_bias)
    hidden = jnp.pad(hidden, ((1, 1), (0, 0), (1, 1), (1, 1)), mode="wrap")
    weights = conv_weight.astype(jnp.float32)
    biases = conv_bias.astype(jnp.float32)
    header = head_weight.astype(jnp.float32)
    ylen = hidden.shape[2] - 2
    zlen = hidden.shape[3] - 2

    def plane(index):
        window = lax.dynamic_slice_in_dim(hidden, index, 3, 0)
        total = jnp.zeros((weights.shape[1], ylen, zlen), jnp.float32)
        for shift_x in range(3):
            for shift_y in range(3):
                for shift_z in range(3):
                    offset = 9 * shift_x + 3 * shift_y + shift_z
                    piece = window[shift_x, :, shift_y:shift_y + ylen, shift_z:shift_z + zlen]
                    total = total + jnp.einsum("oi,iyz->oyz", weights[offset], piece, precision=lax.Precision.HIGHEST)
        activation = jax.nn.silu(total + biases[:, None, None])
        return jnp.einsum("so,oyz->syz", header, activation, precision=lax.Precision.HIGHEST)

    stress = lax.map(plane, jnp.arange(hidden.shape[0] - 2, dtype=jnp.int32))
    flux = fluxes(velocity, upsample(stress))
    along_x = derive(flux, 0)
    along_y = derive(flux, 2)
    along_z = derive(flux, 3)
    first = along_x[:, 0] + along_y[:, 3] + along_z[:, 4]
    second = along_x[:, 3] + along_y[:, 1] + along_z[:, 5]
    third = along_x[:, 4] + along_y[:, 5] + along_z[:, 2]
    divergence = jnp.stack([first, second, third], axis=1)
    return velocity - step_size * divergence, stress
```

```python
import jax
import jax.numpy as jnp
from jax import lax
from jax.experimental import pallas as pl
from jax.experimental.pallas import tpu as pltpu
from jax.sharding import PartitionSpec as P

MESH = pl.DeviceIdType.MESH
F32 = jnp.float32
BF16 = jnp.bfloat16
NROW, NCOL, NCHAN = 16, 12, 4
ZROWS = 144
COEFS = ((1, 45.0), (2, -9.0), (3, 1.0))
X_COMPS = (0, 3, 4)
Y_COMPS = (3, 1, 5)
Z_COMPS = (4, 5, 2)

PEERS = [
    (dr, dc, dx)
    for dr in (-1, 0, 1)
    for dc in (-1, 0, 1)
    for dx in (-1, 0, 1)
    if (dr, dc, dx) != (0, 0, 0)
] + [(0, 0, 2)]


def iota(shape, dim):
    return lax.broadcasted_iota(jnp.int32, shape, dim)


def split(value):
    high = value.astype(BF16)
    return high, (value - high.astype(F32)).astype(BF16)


def split3(value):
    high = value.astype(BF16)
    rest = value - high.astype(F32)
    mid = rest.astype(BF16)
    return high, mid, (rest - mid.astype(F32)).astype(BF16)


def mm(a, b, dims=((1,), (0,)), exact=False):
    return lax.dot_general(
        a,
        b,
        (dims, ((), ())),
        preferred_element_type=F32,
        precision=lax.Precision.HIGHEST if exact else None,
    )


NT = ((1,), (1,))
TN = ((0,), (0,))


def mm2(value, matrix):
    high, low = split(value)
    rows = value.shape[0]
    both = mm(jnp.concatenate([high, low], 0), matrix)
    return both[:rows] + both[rows:]


def stencil_matrix(distance):
    total = jnp.zeros(distance.shape, F32)
    for k, c in COEFS:
        total = jnp.where(distance == k, c, jnp.where(distance == -k, -c, total))
    return total.astype(BF16)


def body_kernel(
    vel_in, lift_w_in, lift_b_in, conv_w_in, conv_b_in, head_w_in,
    out, stress_out,
    vel, lift_w, lift_b, conv_w, conv_b, head_w,
    xs, bx, ysend, csend, zvsend, yvsend, yvstage, wall,
    yland, cland, xland, zvland, yvland, xv, stx, sland,
    hid, taps, headk, strs, field, edge, base, e2, zd,
    send_sem, recv_sem, load_sem,
):
    here = (lax.axis_index("row"), lax.axis_index("col"), lax.axis_index("chan"))
    me = here[2]

    def peer(off):
        return tuple(
            h if o == 0 else lax.rem(h + (o + n) % n, n)
            for h, o, n in zip(here, off, (NROW, NCOL, NCHAN))
        )

    barrier = pltpu.get_barrier_semaphore()
    for off in PEERS:
        pl.semaphore_signal(barrier, inc=1, device_id=peer(off), device_id_type=MESH)

    pairs_in = (
        (vel_in, vel), (conv_w_in, conv_w), (lift_w_in, lift_w), (lift_b_in, lift_b),
        (conv_b_in, conv_b), (head_w_in, head_w),
    )
    loads = [
        pltpu.make_async_copy(src, dst, load_sem.at[k]) for k, (src, dst) in enumerate(pairs_in)
    ]
    for load in loads:
        load.start()
    copies = []

    def send(src, dst, source, landed=None):
        k = len(copies)
        copy = pltpu.make_async_remote_copy(
            src_ref=src, dst_ref=dst, send_sem=send_sem.at[k], recv_sem=recv_sem.at[k],
            device_id=peer(tuple(-s for s in source)), device_id_type=MESH,
        )
        copy.start()
        if landed is not None:
            copies.append((copy, pltpu.make_async_remote_copy(
                src_ref=src, dst_ref=landed, send_sem=send_sem.at[k], recv_sem=recv_sem.at[k],
                device_id=peer(tuple(-s for s in source)), device_id_type=MESH,
            )))
        else:
            copies.append((copy, copy))
        return k

    def arrive(ks):
        for k in ks:
            copies[k][1].wait_recv()

    pool = jnp.where(iota((256, 128), 0) // 2 == iota((256, 128), 1), 1.0, 0.0).astype(BF16)
    r16 = iota((16, 256), 0)
    ends = jnp.where(r16 < 4, r16, r16 + 120)
    picker = jnp.where((iota((16, 256), 1) // 2 == ends) & (r16 < 8), 1.0, 0.0).astype(BF16)
    csend[...] = jnp.zeros_like(csend)
    loads[0].wait()
    for p in range(2):
        for c in range(3):
            both = vel[2 * p, c] + vel[2 * p + 1, c]
            r = 16 * (3 * p + c)
            xs[0, r : r + 16, :] = both[:, :128]
            xs[1, r : r + 16, :] = both[:, 128:]
    pairs = jnp.concatenate(
        [xs[h, pl.ds(0, 48, 2), :] + xs[h, pl.ds(1, 48, 2), :] for h in range(2)], axis=1
    )
    pieces = split3(pairs * 0.125)
    pooled = mm(jnp.concatenate(pieces, 0), pool)
    box = pooled[0:48] + pooled[48:96] + pooled[96:144]
    bx[0] = box[0:24]
    bx[1] = box[24:48]
    for p in range(2):
        for c in range(3):
            r = 8 * (3 * p + c)
            ysend[0, p, c] = box[r + 4 : r + 8]
            ysend[1, p, c] = box[r : r + 4]
    columns = mm(picker, pieces[0], NT) + mm(picker, pieces[1], NT) + mm(picker, pieces[2], NT)
    csend[0, :, 0:48] = columns[4:8]
    csend[1, :, 0:48] = columns[0:4]
    for k in range(12):
        yvstage[0, 4 * k : 4 * k + 4, :] = vel[k // 3, k % 3, 12:16, :]
        yvstage[1, 4 * k : 4 * k + 4, :] = vel[k // 3, k % 3, 0:4, :]
    slot = iota((48, 256), 0) % 4
    for s, near, spare in ((0, 3, 0), (1, 0, 3)):
        high, low = split(yvstage[s])
        moved = pltpu.roll(low.astype(F32), (spare - near) % 48, 0)
        yvsend[s] = jnp.where(slot == spare, moved, high.astype(F32)).astype(BF16)

    pl.semaphore_wait(barrier, len(PEERS))

    ybox, corner, ycols, yvel = [], [], [], []
    for s, dr in ((0, -1), (1, 1)):
        ybox.append(send(ysend.at[s], yland.at[s, 1:3], (dr, 0, 0)))
    for s, dr in ((0, -1), (1, 1)):
        ybox.append(send(ysend.at[s, 1], yland.at[s, 0], (dr, 0, -1)))
        ybox.append(send(ysend.at[s, 0], yland.at[s, 3], (dr, 0, 1)))
    for s, dr in ((1, -1), (2, 1)):
        for t, dc in ((0, -1), (1, 1)):
            for dx in (-1, 0, 1):
                corner.append(send(csend.at[t], cland.at[s, t, dx + 1], (dr, dc, dx)))
    for t, dc in ((0, -1), (1, 1)):
        for dx in (-1, 0, 1):
            ycols.append(send(csend.at[t], cland.at[0, t, dx + 1], (0, dc, dx)))
    xbox = [send(bx.at[1], xland.at[0], (0, 0, -1)), send(bx.at[0], xland.at[1], (0, 0, 1))]
    for s, dr in ((0, -1), (1, 1)):
        yvel.append(send(yvsend.at[s], yvland.at[s], (dr, 0, 0)))

    for load in loads[1:]:
        load.wait()
    for k in range(9):
        a, c = k // 3, k % 3
        parts = [conv_w[9 * a + 3 * b + c].astype(F32) for b in range(3)]
        wall[me, 8 * k : 8 * k + 8, :] = jnp.concatenate(parts + [jnp.zeros((8, 32), F32)], axis=1)
    wall[me, 72:80, :] = jnp.zeros((8, 128), F32)
    wall[me, 72:78, 0:8] = head_w[...].astype(F32)
    wall[me, 78:79, 0:8] = conv_b[...].astype(F32)
    weights = [
        send(wall.at[me], wall.at[me], (0, 0, dx), wall.at[lax.rem(me + (dx + 4) % 4, 4)])
        for dx in (-1, 1, 2)
    ]
    rz = iota((16, 256), 0)
    at = jnp.where(rz < 8, rz + 248, rz - 8)
    take = jnp.where(iota((16, 256), 1) == at, 1.0, 0.0)
    zvsend[...] = jnp.zeros_like(zvsend)
    for c in range(3):
        cols = mm(take, vel[:, c].reshape(64, 256), NT, exact=True)
        zvsend[0, c, :, 0:64] = cols[0:8]
        zvsend[1, c, :, 0:64] = cols[8:16]
    zvel = [send(zvsend.at[t], zvland.at[t], (0, dc, 0)) for t, dc in ((0, -1), (1, 1))]
    xvel = [send(vel.at[1:4], xv.at[0], (0, 0, -1)), send(vel.at[0:3], xv.at[1], (0, 0, 1))]

    spread = jnp.where(iota((32, 256), 1) % 32 == iota((32, 256), 0), 1.0, 0.0)
    bias = mm(lift_b[...], spread, exact=True)
    rows24 = jnp.where(iota((24, 3), 0) // 8 == iota((24, 3), 1), 1.0, 0.0)
    lift = mm(rows24, mm(lift_w[...], spread, exact=True), exact=True)
    lift = jnp.where(iota((24, 256), 0) % 8 == iota((24, 256), 1) // 32, lift, 0.0)
    lift_of = [
        jnp.concatenate([lift, jnp.zeros((104, 256), F32)], 0),
        jnp.concatenate([jnp.zeros((24, 256), F32), lift, jnp.zeros((80, 256), F32)], 0),
    ]

    def hold(q, row, lane, value):
        high, low = split(value)
        n, m = value.shape
        hid[q, row : row + n, lane : lane + m] = high
        hid[q, ZROWS + row : ZROWS + row + n, lane : lane + m] = low

    def lifted(rows):
        return jnp.tanh(mm(rows, lift, TN, exact=True) + bias)

    def side(s, dx):
        return jnp.concatenate(
            [cland[s, 1, dx + 1], jnp.zeros((8, 128), F32), cland[s, 0, dx + 1]], 0
        )

    PLANES = ((0, -1, 1), (1, 0, 0), (2, 0, 1), (3, 1, 0))
    for p in range(2):
        hold(p + 1, 0, 128, lifted(bx[p]))
    arrive(xbox)
    hold(0, 0, 128, lifted(xland[0]))
    hold(3, 0, 128, lifted(xland[1]))

    arrive(weights)
    lane = iota((32, 128), 1)
    zero = jnp.zeros((32, 128), F32)
    for k in range(9):
        a, c = k // 3, k % 3
        x = jnp.concatenate([wall[n, 8 * k : 8 * k + 8, :] for n in range(4)], 0)
        r1, r2, r3 = (pltpu.roll(x, 32 * n, 1) for n in (1, 2, 3))
        tiles = (
            (r1, zero),
            (jnp.where(lane >= 64, r2, 0.0), jnp.where(lane < 64, r2, 0.0)),
            (jnp.where(lane >= 96, r3, 0.0), jnp.where(lane < 96, r3, 0.0)),
            (zero, x),
        )
        for y, (first, second) in enumerate(tiles):
            r = 128 * c + 32 * y
            taps[a, r : r + 32, 0:128] = first.astype(BF16)
            taps[a, r : r + 32, 128:256] = second.astype(BF16)
    params = wall[0, 72:80, :]
    for n in range(1, 4):
        params = params + pltpu.roll(wall[n, 72:80, :], 8 * n, 1)
    rolled = [params] + [pltpu.roll(params, 32 * n, 1) for n in (1, 2, 3)]
    conv_bias = (rolled[0] + rolled[1] + rolled[2] + rolled[3])[6:7]
    for n in range(4):
        headk[pl.ds(n, 8, 4), :] = rolled[n]
    head = headk[...].astype(BF16)

    arrive(ycols)
    for q, dx, p in PLANES:
        hold(q, 128, 128, jnp.tanh(mm(side(0, dx), lift_of[p], exact=True) + bias))

    def closure(g):
        total = None
        for a in range(3):
            block = hid[a : a + 2, :, 128 * g : 128 * g + 256].reshape(4 * ZROWS, 256)
            term = mm(block, taps[a], NT)
            total = term if total is None else total + term
        for p in range(2):
            r = 2 * ZROWS * p
            both = total[r : r + ZROWS] + total[r + ZROWS : r + 2 * ZROWS]
            conv = (
                pltpu.roll(both[:, 0:128], 1, 0)
                + both[:, 128:256]
                + pltpu.roll(both[:, 256:384], ZROWS - 1, 0)
                + conv_bias
            )
            act = 0.5 * conv * (1.0 + jnp.tanh(0.5 * conv))
            high, low = split(act)
            found = mm(head, high, NT) + mm(head, low, NT)
            for s in range(6):
                strs[p, s, 4 * g : 4 * g + 4, 0:ZROWS] = found[4 * s : 4 * s + 4]

    closure(1)

    field[...] = jnp.zeros_like(field)
    for p in range(4):
        uy = vel[p, 1]
        for i in range(3):
            field[p, i, 8:24, :] = uy * vel[p, i]
    stencil = stencil_matrix(iota((256, 256), 0) - iota((256, 256), 1))
    for i in range(3):
        flux = (vel[:, 2] * vel[:, i]).reshape(64, 256)
        base[:, i] = mm2(flux, stencil).reshape(4, 16, 256)
    for p in range(4):
        for i in range(3):
            total = base[p, i]
            for k, c in COEFS:
                total = total + c * (field[p, i, 8 + k : 24 + k, :] - field[p, i, 8 - k : 24 - k, :])
            base[p, i] = total
    arrive(zvel)
    r16z = iota((16, 256), 0)
    place = jnp.where(r16z < 8, r16z - 8, r16z + 248)
    rim = stencil_matrix(place - iota((16, 256), 1)).astype(F32)
    cols = [jnp.concatenate([zvland[0, c], zvland[1, c]], 0)[:, 0:64] for c in range(3)]
    for i in range(3):
        base[:, i] += mm(cols[2] * cols[i], rim, TN, exact=True).reshape(4, 16, 256)
    arrive(xvel)
    for i in range(3):
        planes = (
            [xv[0, n, 0] * xv[0, n, i] for n in range(3)]
            + [vel[n, 0] * vel[n, i] for n in range(4)]
            + [xv[1, n, 0] * xv[1, n, i] for n in range(3)]
        )
        for p in range(4):
            total = base[p, i]
            for k, c in COEFS:
                total = total + c * (planes[p + 3 + k] - planes[p + 3 - k])
            base[p, i] = total

    arrive(ybox)
    for q in range(4):
        rows = jnp.concatenate(
            [jnp.concatenate([yland[1, q, c], yland[0, q, c]], 0) for c in range(3)], 0
        )
        h = lifted(rows)
        hold(q, 0, 0, h[:, 128:256])
        hold(q, 0, 384, h[:, 0:128])
    arrive(corner)
    for q, dx, p in PLANES:
        rows = jnp.concatenate([side(1, dx), side(2, dx)], 0)
        h = jnp.tanh(mm(rows, lift_of[p], exact=True) + bias)
        hold(q, 128, 0, h[0:16, 128:256])
        hold(q, 128, 384, h[16:32, 0:128])
    closure(0)
    closure(2)

    for p in range(2):
        for i, s in enumerate(X_COMPS):
            stx[p, i] = strs[p, s, 2:10, 0:128]
    xstress = [send(stx, sland.at[0], (0, 0, -1)), send(stx, sland.at[1], (0, 0, 1))]

    for p in range(2):
        for s in range(6):
            stress_out[p, s] = strs[p, s, 2:10, 0:128]

    arrive(yvel)
    edge[...] = jnp.zeros_like(edge)
    both_sides = []
    for s, near, spare in ((0, 3, 0), (1, 0, 3)):
        rows = yvland[s].astype(F32)
        low = pltpu.roll(rows, (near - spare) % 48, 0)
        both_sides.append(rows + jnp.where(slot == near, low, 0.0))
    above, below = both_sides
    for p in range(4):
        for i in range(3):
            k, y, n = 4 * (3 * p + i), 4 * (3 * p + 1), 3 * p + i
            edge[n, 4:8, :] = above[y : y + 4] * above[k : k + 4]
            edge[n, 16:20, :] = below[y : y + 4] * below[k : k + 4]
    for p in range(4):
        for i in range(3):
            n = 3 * p + i
            top = base[p, i, 0:8]
            bottom = base[p, i, 8:16]
            for k, c in COEFS:
                top = top - c * edge[n, 8 - k : 16 - k, :]
                bottom = bottom + c * edge[n, 8 + k : 16 + k, :]
            base[p, i, 0:8] = top
            base[p, i, 8:16] = bottom

    l144, c256 = iota((ZROWS, 256), 0), iota((ZROWS, 256), 1)
    dist = jnp.where(l144 < 136, l144, l144 - ZROWS) - c256 // 2
    even = jnp.where(dist == 0, 45.0, jnp.where(dist == -1, -36.0, jnp.where(dist == 1, -8.0, jnp.where(dist == -2, -1.0, 0.0))))
    odd = jnp.where(dist == 1, 36.0, jnp.where(dist == 0, -45.0, jnp.where(dist == -1, 8.0, jnp.where(dist == 2, 1.0, 0.0))))
    along = jnp.where(c256 % 2 == 0, even, odd).astype(BF16)
    zrows = jnp.concatenate(
        [strs[p, s, 2:10, 0:ZROWS] for p in range(2) for s in Z_COMPS], 0
    )
    zder = mm2(zrows, along)
    for p in range(2):
        for i in range(3):
            r = 8 * (3 * p + i)
            for half in range(2):
                piece = zder[r : r + 8, 128 * half : 128 * half + 128]
                zd[p, i, half, pl.ds(0, 8, 2), :] = piece
                zd[p, i, half, pl.ds(1, 8, 2), :] = piece
    yder = []
    for p in range(2):
        for i, s in enumerate(Y_COMPS):
            c = {k: strs[p, s, 2 + k : 10 + k, 0:128] for k in range(-2, 3)}
            yder.append((
                45.0 * c[0] - 36.0 * c[-1] - 8.0 * c[1] - c[-2],
                36.0 * c[1] - 45.0 * c[0] + 8.0 * c[-1] + c[2],
            ))
    double = jnp.where(iota((128, 256), 1) // 2 == iota((128, 256), 0), 1.0, 0.0).astype(BF16)

    arrive(xstress)
    for i in range(3):
        c = [sland[0, 0, i], sland[0, 1, i], stx[0, i], stx[1, i], sland[1, 0, i], sland[1, 1, i]]
        for p in range(2):
            n = p + 2
            xder = (
                45.0 * c[n] - 36.0 * c[n - 1] - 8.0 * c[n + 1] - c[n - 2],
                36.0 * c[n + 1] - 45.0 * c[n] + 8.0 * c[n - 1] + c[n + 2],
            )
            for px in range(2):
                for py in range(2):
                    e2[2 * p + px, i, pl.ds(py, 8, 2), :] = xder[px] + yder[3 * p + i][py]
    fine = mm2(e2[...].reshape(192, 128), double)
    for p in range(4):
        for i in range(3):
            r = 16 * (3 * p + i)
            zpart = jnp.concatenate([zd[p // 2, i, 0], zd[p // 2, i, 1]], axis=1)
            total = base[p, i] + fine[r : r + 16] + zpart
            out[p, i] = vel[p, i] - (0.1 / 60.0) * total

    for copy, _ in copies:
        copy.wait_send()


def body(velocity, lift_weight, lift_bias, conv_weight, conv_bias, head_weight):
    vmem = pl.BlockSpec(memory_space=pltpu.VMEM)
    ncopies = 6 + 12 + 6 + 2 + 2 + 3 + 2 + 2 + 2
    scratch = [
        pltpu.VMEM((4, 3, 16, 256), F32),
        pltpu.VMEM((3, 32), F32),
        pltpu.VMEM((1, 32), F32),
        pltpu.VMEM((27, 8, 32), BF16),
        pltpu.VMEM((1, 8), BF16),
        pltpu.VMEM((6, 8), BF16),
        pltpu.VMEM((2, 96, 128), F32),
        pltpu.VMEM((2, 24, 128), F32),
        pltpu.VMEM((2, 2, 3, 4, 128), F32),
        pltpu.VMEM((2, 4, 128), F32),
        pltpu.VMEM((2, 3, 8, 128), F32),
        pltpu.VMEM((2, 48, 256), BF16),
        pltpu.VMEM((2, 48, 256), F32),
        pltpu.VMEM((4, 80, 128), F32),
        pltpu.VMEM((2, 4, 3, 4, 128), F32),
        pltpu.VMEM((3, 2, 3, 4, 128), F32),
        pltpu.VMEM((2, 24, 128), F32),
        pltpu.VMEM((2, 3, 8, 128), F32),
        pltpu.VMEM((2, 48, 256), BF16),
        pltpu.VMEM((2, 3, 3, 16, 256), F32),
        pltpu.VMEM((2, 3, 8, 128), F32),
        pltpu.VMEM((2, 2, 3, 8, 128), F32),
        pltpu.VMEM((4, 2 * ZROWS, 512), BF16),
        pltpu.VMEM((3, 384, 256), BF16),
        pltpu.VMEM((32, 128), F32),
        pltpu.VMEM((2, 6, 16, 256), F32),
        pltpu.VMEM((4, 3, 32, 256), F32),
        pltpu.VMEM((12, 24, 256), F32),
        pltpu.VMEM((4, 3, 16, 256), F32),
        pltpu.VMEM((4, 3, 16, 128), F32),
        pltpu.VMEM((2, 3, 2, 16, 128), F32),
        pltpu.SemaphoreType.DMA((ncopies,)),
        pltpu.SemaphoreType.DMA((ncopies,)),
        pltpu.SemaphoreType.DMA((6,)),
    ]
    return pl.pallas_call(
        body_kernel,
        out_shape=(
            jax.ShapeDtypeStruct((4, 3, 16, 256), F32),
            jax.ShapeDtypeStruct((2, 6, 8, 128), F32),
        ),
        in_specs=[pl.BlockSpec(memory_space=pltpu.HBM)] * 6,
        out_specs=(vmem, vmem),
        scratch_shapes=scratch,
        compiler_params=pltpu.CompilerParams(
            collective_id=0, has_side_effects=True, vmem_limit_bytes=40 * 2**20
        ),
    )(
        velocity,
        lift_weight.T,
        lift_bias.reshape(1, 32),
        conv_weight,
        conv_bias.reshape(1, 8),
        head_weight,
    )


def solution(mesh):
    placed = (
        P("chan", None, "row", "col"),
        P(),
        P(),
        P(None, "chan", None),
        P("chan"),
        P(None, "chan"),
    )
    return jax.shard_map(
        body,
        mesh=mesh,
        in_specs=placed,
        out_specs=(P("chan", None, "row", "col"), P("chan", None, "row", "col")),
        check_vma=False,
    )
```

```python
import jax
import jax.numpy as jnp
from jax import lax
from jax.experimental import pallas as pl
from jax.experimental.pallas import tpu as pltpu
from jax.sharding import PartitionSpec as P

MESH = pl.DeviceIdType.MESH
F32 = jnp.float32
BF16 = jnp.bfloat16
NROW, NCOL, NCHAN = 16, 12, 4
ZROWS = 144
COEFS = ((1, 45.0), (2, -9.0), (3, 1.0))
X_COMPS = (0, 3, 4)
Y_COMPS = (3, 1, 5)
Z_COMPS = (4, 5, 2)

NEAR = [(0, dc, dx) for dc in (-1, 0, 1) for dx in (-1, 0, 1) if (dc, dx) != (0, 0)] + [(0, 0, 2)]
FAR = [(dr, dc, dx) for dr in (-1, 1) for dc in (-1, 0, 1) for dx in (-1, 0, 1)]


def iota(shape, dim):
    return lax.broadcasted_iota(jnp.int32, shape, dim)


def split(value):
    high = value.astype(BF16)
    return high, (value - high.astype(F32)).astype(BF16)


def split3(value):
    high = value.astype(BF16)
    rest = value - high.astype(F32)
    mid = rest.astype(BF16)
    return high, mid, (rest - mid.astype(F32)).astype(BF16)


def mm(a, b, dims=((1,), (0,)), exact=False):
    return lax.dot_general(
        a,
        b,
        (dims, ((), ())),
        preferred_element_type=F32,
        precision=lax.Precision.HIGHEST if exact else None,
    )


NT = ((1,), (1,))
TN = ((0,), (0,))


def mm2(value, matrix):
    high, low = split(value)
    rows = value.shape[0]
    both = mm(jnp.concatenate([high, low], 0), matrix)
    return both[:rows] + both[rows:]


def stencil_matrix(distance):
    total = jnp.zeros(distance.shape, F32)
    for k, c in COEFS:
        total = jnp.where(distance == k, c, jnp.where(distance == -k, -c, total))
    return total.astype(BF16)


def body_kernel(
    vel_in, lift_w_in, lift_b_in, conv_w_in, conv_b_in, head_w_in,
    out, stress_out,
    vel, lift_w, lift_b, conv_w, conv_b, head_w,
    xs, bx, ysend, csend, zvsend, yvsend, yvstage, wall,
    yland, cland, xland, zvland, yvland, xv, stx, sland,
    hid, taps, headk, strs, field, edge, base, e2, zd,
    send_sem, recv_sem, load_sem, ready,
):
    here = (lax.axis_index("row"), lax.axis_index("col"), lax.axis_index("chan"))
    me = here[2]

    def peer(off):
        return tuple(
            h if o == 0 else lax.rem(h + (o + n) % n, n)
            for h, o, n in zip(here, off, (NROW, NCOL, NCHAN))
        )

    odd = lax.rem(here[0], 2)
    barrier = pltpu.get_barrier_semaphore()
    for off in NEAR:
        pl.semaphore_signal(barrier, inc=1, device_id=peer(off), device_id_type=MESH)

    @pl.when(odd == 0)
    def _():
        for off in FAR:
            pl.semaphore_signal(barrier, inc=1, device_id=peer(off), device_id_type=MESH)


    pairs_in = (
        (vel_in, vel), (conv_w_in, conv_w), (lift_w_in, lift_w), (lift_b_in, lift_b),
        (conv_b_in, conv_b), (head_w_in, head_w),
    )
    loads = [
        pltpu.make_async_copy(src, dst, load_sem.at[k]) for k, (src, dst) in enumerate(pairs_in)
    ]
    for load in loads:
        load.start()
    copies = []

    def send(src, dst, source, landed=None, start=True):
        k = len(copies)
        copy = pltpu.make_async_remote_copy(
            src_ref=src, dst_ref=dst, send_sem=send_sem.at[k], recv_sem=recv_sem.at[k],
            device_id=peer(tuple(-s for s in source)), device_id_type=MESH,
        )
        if start:
            copy.start()
        if landed is not None:
            copies.append((copy, pltpu.make_async_remote_copy(
                src_ref=src, dst_ref=landed, send_sem=send_sem.at[k], recv_sem=recv_sem.at[k],
                device_id=peer(tuple(-s for s in source)), device_id_type=MESH,
            )))
        else:
            copies.append((copy, copy))
        return k

    def arrive(ks):
        for k in ks:
            copies[k][1].wait_recv()

    pool = jnp.where(iota((256, 128), 0) // 2 == iota((256, 128), 1), 1.0, 0.0).astype(BF16)
    r16 = iota((16, 256), 0)
    ends = jnp.where(r16 < 4, r16, r16 + 120)
    picker = jnp.where((iota((16, 256), 1) // 2 == ends) & (r16 < 8), 1.0, 0.0).astype(BF16)
    csend[...] = jnp.zeros_like(csend)
    loads[0].wait()
    for p in range(2):
        for c in range(3):
            both = vel[2 * p, c] + vel[2 * p + 1, c]
            r = 16 * (3 * p + c)
            xs[0, r : r + 16, :] = both[:, :128]
            xs[1, r : r + 16, :] = both[:, 128:]
    pairs = jnp.concatenate(
        [xs[h, pl.ds(0, 48, 2), :] + xs[h, pl.ds(1, 48, 2), :] for h in range(2)], axis=1
    )
    pieces = split3(pairs * 0.125)
    pooled = mm(jnp.concatenate(pieces, 0), pool)
    box = pooled[0:48] + pooled[48:96] + pooled[96:144]
    bx[0] = box[0:24]
    bx[1] = box[24:48]
    for p in range(2):
        for c in range(3):
            r = 8 * (3 * p + c)
            ysend[0, p, c] = box[r + 4 : r + 8]
            ysend[1, p, c] = box[r : r + 4]
    columns = mm(picker, pieces[0], NT) + mm(picker, pieces[1], NT) + mm(picker, pieces[2], NT)
    csend[0, :, 0:48] = columns[4:8]
    csend[1, :, 0:48] = columns[0:4]
    for k in range(12):
        yvstage[0, 4 * k : 4 * k + 4, :] = vel[k // 3, k % 3, 12:16, :]
        yvstage[1, 4 * k : 4 * k + 4, :] = vel[k // 3, k % 3, 0:4, :]
    slot = iota((48, 256), 0) % 4
    for s, near, spare in ((0, 3, 0), (1, 0, 3)):
        high, low = split(yvstage[s])
        moved = pltpu.roll(low.astype(F32), (spare - near) % 48, 0)
        yvsend[s] = jnp.where(slot == spare, moved, high.astype(F32)).astype(BF16)

    pl.semaphore_wait(barrier, len(NEAR) + len(FAR) * odd)

    ybox, corner, ycols, yvel = [], [], [], []
    for s, dr in ((0, -1), (1, 1)):
        ybox.append(send(ysend.at[s], yland.at[s, 1:3], (dr, 0, 0), start=False))
        ybox.append(send(ysend.at[s, 1], yland.at[s, 0], (dr, 0, -1), start=False))
        ybox.append(send(ysend.at[s, 0], yland.at[s, 3], (dr, 0, 1), start=False))
    for s, dr in ((1, -1), (2, 1)):
        for t, dc in ((0, -1), (1, 1)):
            for dx in (-1, 0, 1):
                corner.append(
                    send(csend.at[t], cland.at[s, t, dx + 1], (dr, dc, dx), start=False)
                )
    for s, dr in ((0, -1), (1, 1)):
        yvel.append(send(yvsend.at[s], yvland.at[s], (dr, 0, 0), start=False))
    far_copies = [copies[k][0] for k in ybox + corner + yvel]

    @pl.when(odd == 1)
    def _():
        for copy in far_copies:
            copy.start()
        for off in FAR:
            pl.semaphore_signal(ready, inc=1, device_id=peer(off), device_id_type=MESH)

    for t, dc in ((0, -1), (1, 1)):
        for dx in (-1, 0, 1):
            ycols.append(send(csend.at[t], cland.at[0, t, dx + 1], (0, dc, dx)))
    xbox = [send(bx.at[1], xland.at[0], (0, 0, -1)), send(bx.at[0], xland.at[1], (0, 0, 1))]

    for load in loads[1:]:
        load.wait()
    for k in range(9):
        a, c = k // 3, k % 3
        parts = [conv_w[9 * a + 3 * b + c].astype(F32) for b in range(3)]
        wall[me, 8 * k : 8 * k + 8, :] = jnp.concatenate(parts + [jnp.zeros((8, 32), F32)], axis=1)
    wall[me, 72:80, :] = jnp.zeros((8, 128), F32)
    wall[me, 72:78, 0:8] = head_w[...].astype(F32)
    wall[me, 78:79, 0:8] = conv_b[...].astype(F32)
    weights = [
        send(wall.at[me], wall.at[me], (0, 0, dx), wall.at[lax.rem(me + (dx + 4) % 4, 4)])
        for dx in (-1, 1, 2)
    ]
    rz = iota((16, 256), 0)
    at = jnp.where(rz < 8, rz + 248, rz - 8)
    take = jnp.where(iota((16, 256), 1) == at, 1.0, 0.0)
    zvsend[...] = jnp.zeros_like(zvsend)
    for c in range(3):
        cols = mm(take, vel[:, c].reshape(64, 256), NT, exact=True)
        zvsend[0, c, :, 0:64] = cols[0:8]
        zvsend[1, c, :, 0:64] = cols[8:16]
    zvel = [send(zvsend.at[t], zvland.at[t], (0, dc, 0)) for t, dc in ((0, -1), (1, 1))]
    xvel = [send(vel.at[1:4], xv.at[0], (0, 0, -1)), send(vel.at[0:3], xv.at[1], (0, 0, 1))]

    spread = jnp.where(iota((32, 256), 1) % 32 == iota((32, 256), 0), 1.0, 0.0)
    bias = mm(lift_b[...], spread, exact=True)
    rows24 = jnp.where(iota((24, 3), 0) // 8 == iota((24, 3), 1), 1.0, 0.0)
    lift = mm(rows24, mm(lift_w[...], spread, exact=True), exact=True)
    lift = jnp.where(iota((24, 256), 0) % 8 == iota((24, 256), 1) // 32, lift, 0.0)
    lift_of = [
        jnp.concatenate([lift, jnp.zeros((104, 256), F32)], 0),
        jnp.concatenate([jnp.zeros((24, 256), F32), lift, jnp.zeros((80, 256), F32)], 0),
    ]

    def hold(q, row, lane, value):
        high, low = split(value)
        n, m = value.shape
        hid[q, row : row + n, lane : lane + m] = high
        hid[q, ZROWS + row : ZROWS + row + n, lane : lane + m] = low

    def lifted(rows):
        return jnp.tanh(mm(rows, lift, TN, exact=True) + bias)

    def side(s, dx):
        return jnp.concatenate(
            [cland[s, 1, dx + 1], jnp.zeros((8, 128), F32), cland[s, 0, dx + 1]], 0
        )

    PLANES = ((0, -1, 1), (1, 0, 0), (2, 0, 1), (3, 1, 0))
    for p in range(2):
        hold(p + 1, 0, 128, lifted(bx[p]))
    arrive(xbox)
    hold(0, 0, 128, lifted(xland[0]))
    hold(3, 0, 128, lifted(xland[1]))

    arrive(weights)
    lane = iota((32, 128), 1)
    zero = jnp.zeros((32, 128), F32)
    for k in range(9):
        a, c = k // 3, k % 3
        x = jnp.concatenate([wall[n, 8 * k : 8 * k + 8, :] for n in range(4)], 0)
        r1, r2, r3 = (pltpu.roll(x, 32 * n, 1) for n in (1, 2, 3))
        tiles = (
            (r1, zero),
            (jnp.where(lane >= 64, r2, 0.0), jnp.where(lane < 64, r2, 0.0)),
            (jnp.where(lane >= 96, r3, 0.0), jnp.where(lane < 96, r3, 0.0)),
            (zero, x),
        )
        for y, (first, second) in enumerate(tiles):
            r = 128 * c + 32 * y
            taps[a, r : r + 32, 0:128] = first.astype(BF16)
            taps[a, r : r + 32, 128:256] = second.astype(BF16)
    params = wall[0, 72:80, :]
    for n in range(1, 4):
        params = params + pltpu.roll(wall[n, 72:80, :], 8 * n, 1)
    rolled = [params] + [pltpu.roll(params, 32 * n, 1) for n in (1, 2, 3)]
    conv_bias = (rolled[0] + rolled[1] + rolled[2] + rolled[3])[6:7]
    for n in range(4):
        headk[pl.ds(n, 8, 4), :] = rolled[n]
    head = headk[...].astype(BF16)

    arrive(ycols)
    for q, dx, p in PLANES:
        hold(q, 128, 128, jnp.tanh(mm(side(0, dx), lift_of[p], exact=True) + bias))

    def closure(g):
        total = None
        for a in range(3):
            block = hid[a : a + 2, :, 128 * g : 128 * g + 256].reshape(4 * ZROWS, 256)
            term = mm(block, taps[a], NT)
            total = term if total is None else total + term
        for p in range(2):
            r = 2 * ZROWS * p
            both = total[r : r + ZROWS] + total[r + ZROWS : r + 2 * ZROWS]
            conv = (
                pltpu.roll(both[:, 0:128], 1, 0)
                + both[:, 128:256]
                + pltpu.roll(both[:, 256:384], ZROWS - 1, 0)
                + conv_bias
            )
            act = 0.5 * conv * (1.0 + jnp.tanh(0.5 * conv))
            high, low = split(act)
            found = mm(head, high, NT) + mm(head, low, NT)
            for s in range(6):
                strs[p, s, 4 * g : 4 * g + 4, 0:ZROWS] = found[4 * s : 4 * s + 4]

    closure(1)

    field[...] = jnp.zeros_like(field)
    for p in range(4):
        uy = vel[p, 1]
        for i in range(3):
            field[p, i, 8:24, :] = uy * vel[p, i]
    stencil = stencil_matrix(iota((256, 256), 0) - iota((256, 256), 1))
    for i in range(3):
        flux = (vel[:, 2] * vel[:, i]).reshape(64, 256)
        base[:, i] = mm2(flux, stencil).reshape(4, 16, 256)
    for p in range(4):
        for i in range(3):
            total = base[p, i]
            for k, c in COEFS:
                total = total + c * (field[p, i, 8 + k : 24 + k, :] - field[p, i, 8 - k : 24 - k, :])
            base[p, i] = total
    arrive(zvel)
    r16z = iota((16, 256), 0)
    place = jnp.where(r16z < 8, r16z - 8, r16z + 248)
    rim = stencil_matrix(place - iota((16, 256), 1)).astype(F32)
    cols = [jnp.concatenate([zvland[0, c], zvland[1, c]], 0)[:, 0:64] for c in range(3)]
    for i in range(3):
        base[:, i] += mm(cols[2] * cols[i], rim, TN, exact=True).reshape(4, 16, 256)
    arrive(xvel)
    for i in range(3):
        planes = (
            [xv[0, n, 0] * xv[0, n, i] for n in range(3)]
            + [vel[n, 0] * vel[n, i] for n in range(4)]
            + [xv[1, n, 0] * xv[1, n, i] for n in range(3)]
        )
        for p in range(4):
            total = base[p, i]
            for k, c in COEFS:
                total = total + c * (planes[p + 3 + k] - planes[p + 3 - k])
            base[p, i] = total

    @pl.when(odd == 0)
    def _():
        pl.semaphore_wait(ready, len(FAR))
        for copy in far_copies:
            copy.start()

    arrive(ybox)
    for q in range(4):
        rows = jnp.concatenate(
            [jnp.concatenate([yland[1, q, c], yland[0, q, c]], 0) for c in range(3)], 0
        )
        h = lifted(rows)
        hold(q, 0, 0, h[:, 128:256])
        hold(q, 0, 384, h[:, 0:128])
    arrive(corner)
    for q, dx, p in PLANES:
        rows = jnp.concatenate([side(1, dx), side(2, dx)], 0)
        h = jnp.tanh(mm(rows, lift_of[p], exact=True) + bias)
        hold(q, 128, 0, h[0:16, 128:256])
        hold(q, 128, 384, h[16:32, 0:128])
    closure(0)
    closure(2)

    for p in range(2):
        for i, s in enumerate(X_COMPS):
            stx[p, i] = strs[p, s, 2:10, 0:128]
    xstress = [send(stx, sland.at[0], (0, 0, -1)), send(stx, sland.at[1], (0, 0, 1))]

    for p in range(2):
        for s in range(6):
            stress_out[p, s] = strs[p, s, 2:10, 0:128]

    arrive(yvel)
    edge[...] = jnp.zeros_like(edge)
    both_sides = []
    for s, near, spare in ((0, 3, 0), (1, 0, 3)):
        rows = yvland[s].astype(F32)
        low = pltpu.roll(rows, (near - spare) % 48, 0)
        both_sides.append(rows + jnp.where(slot == near, low, 0.0))
    above, below = both_sides
    for p in range(4):
        for i in range(3):
            k, y, n = 4 * (3 * p + i), 4 * (3 * p + 1), 3 * p + i
            edge[n, 4:8, :] = above[y : y + 4] * above[k : k + 4]
            edge[n, 16:20, :] = below[y : y + 4] * below[k : k + 4]
    for p in range(4):
        for i in range(3):
            n = 3 * p + i
            top = base[p, i, 0:8]
            bottom = base[p, i, 8:16]
            for k, c in COEFS:
                top = top - c * edge[n, 8 - k : 16 - k, :]
                bottom = bottom + c * edge[n, 8 + k : 16 + k, :]
            base[p, i, 0:8] = top
            base[p, i, 8:16] = bottom

    l144, c256 = iota((ZROWS, 256), 0), iota((ZROWS, 256), 1)
    dist = jnp.where(l144 < 136, l144, l144 - ZROWS) - c256 // 2
    even = jnp.where(dist == 0, 45.0, jnp.where(dist == -1, -36.0, jnp.where(dist == 1, -8.0, jnp.where(dist == -2, -1.0, 0.0))))
    odd = jnp.where(dist == 1, 36.0, jnp.where(dist == 0, -45.0, jnp.where(dist == -1, 8.0, jnp.where(dist == 2, 1.0, 0.0))))
    along = jnp.where(c256 % 2 == 0, even, odd).astype(BF16)
    zrows = jnp.concatenate(
        [strs[p, s, 2:10, 0:ZROWS] for p in range(2) for s in Z_COMPS], 0
    )
    zder = mm2(zrows, along)
    for p in range(2):
        for i in range(3):
            r = 8 * (3 * p + i)
            for half in range(2):
                piece = zder[r : r + 8, 128 * half : 128 * half + 128]
                zd[p, i, half, pl.ds(0, 8, 2), :] = piece
                zd[p, i, half, pl.ds(1, 8, 2), :] = piece
    yder = []
    for p in range(2):
        for i, s in enumerate(Y_COMPS):
            c = {k: strs[p, s, 2 + k : 10 + k, 0:128] for k in range(-2, 3)}
            yder.append((
                45.0 * c[0] - 36.0 * c[-1] - 8.0 * c[1] - c[-2],
                36.0 * c[1] - 45.0 * c[0] + 8.0 * c[-1] + c[2],
            ))
    double = jnp.where(iota((128, 256), 1) // 2 == iota((128, 256), 0), 1.0, 0.0).astype(BF16)

    arrive(xstress)
    for i in range(3):
        c = [sland[0, 0, i], sland[0, 1, i], stx[0, i], stx[1, i], sland[1, 0, i], sland[1, 1, i]]
        for p in range(2):
            n = p + 2
            xder = (
                45.0 * c[n] - 36.0 * c[n - 1] - 8.0 * c[n + 1] - c[n - 2],
                36.0 * c[n + 1] - 45.0 * c[n] + 8.0 * c[n - 1] + c[n + 2],
            )
            for px in range(2):
                for py in range(2):
                    e2[2 * p + px, i, pl.ds(py, 8, 2), :] = xder[px] + yder[3 * p + i][py]
    fine = mm2(e2[...].reshape(192, 128), double)
    for p in range(4):
        for i in range(3):
            r = 16 * (3 * p + i)
            zpart = jnp.concatenate([zd[p // 2, i, 0], zd[p // 2, i, 1]], axis=1)
            total = base[p, i] + fine[r : r + 16] + zpart
            out[p, i] = vel[p, i] - (0.1 / 60.0) * total

    for copy, _ in copies:
        copy.wait_send()


def body(velocity, lift_weight, lift_bias, conv_weight, conv_bias, head_weight):
    vmem = pl.BlockSpec(memory_space=pltpu.VMEM)
    ncopies = 6 + 12 + 6 + 2 + 2 + 3 + 2 + 2 + 2
    scratch = [
        pltpu.VMEM((4, 3, 16, 256), F32),
        pltpu.VMEM((3, 32), F32),
        pltpu.VMEM((1, 32), F32),
        pltpu.VMEM((27, 8, 32), BF16),
        pltpu.VMEM((1, 8), BF16),
        pltpu.VMEM((6, 8), BF16),
        pltpu.VMEM((2, 96, 128), F32),
        pltpu.VMEM((2, 24, 128), F32),
        pltpu.VMEM((2, 2, 3, 4, 128), F32),
        pltpu.VMEM((2, 4, 128), F32),
        pltpu.VMEM((2, 3, 8, 128), F32),
        pltpu.VMEM((2, 48, 256), BF16),
        pltpu.VMEM((2, 48, 256), F32),
        pltpu.VMEM((4, 80, 128), F32),
        pltpu.VMEM((2, 4, 3, 4, 128), F32),
        pltpu.VMEM((3, 2, 3, 4, 128), F32),
        pltpu.VMEM((2, 24, 128), F32),
        pltpu.VMEM((2, 3, 8, 128), F32),
        pltpu.VMEM((2, 48, 256), BF16),
        pltpu.VMEM((2, 3, 3, 16, 256), F32),
        pltpu.VMEM((2, 3, 8, 128), F32),
        pltpu.VMEM((2, 2, 3, 8, 128), F32),
        pltpu.VMEM((4, 2 * ZROWS, 512), BF16),
        pltpu.VMEM((3, 384, 256), BF16),
        pltpu.VMEM((32, 128), F32),
        pltpu.VMEM((2, 6, 16, 256), F32),
        pltpu.VMEM((4, 3, 32, 256), F32),
        pltpu.VMEM((12, 24, 256), F32),
        pltpu.VMEM((4, 3, 16, 256), F32),
        pltpu.VMEM((4, 3, 16, 128), F32),
        pltpu.VMEM((2, 3, 2, 16, 128), F32),
        pltpu.SemaphoreType.DMA((ncopies,)),
        pltpu.SemaphoreType.DMA((ncopies,)),
        pltpu.SemaphoreType.DMA((6,)),
        pltpu.SemaphoreType.REGULAR,
    ]
    return pl.pallas_call(
        body_kernel,
        out_shape=(
            jax.ShapeDtypeStruct((4, 3, 16, 256), F32),
            jax.ShapeDtypeStruct((2, 6, 8, 128), F32),
        ),
        in_specs=[pl.BlockSpec(memory_space=pltpu.HBM)] * 6,
        out_specs=(vmem, vmem),
        scratch_shapes=scratch,
        compiler_params=pltpu.CompilerParams(
            collective_id=0, has_side_effects=True, vmem_limit_bytes=60 * 2**20
        ),
    )(
        velocity,
        lift_weight.T,
        lift_bias.reshape(1, 32),
        conv_weight,
        conv_bias.reshape(1, 8),
        head_weight,
    )


def solution(mesh):
    placed = (
        P("chan", None, "row", "col"),
        P(),
        P(),
        P(None, "chan", None),
        P("chan"),
        P(None, "chan"),
    )
    return jax.shard_map(
        body,
        mesh=mesh,
        in_specs=placed,
        out_specs=(P("chan", None, "row", "col"), P("chan", None, "row", "col")),
        check_vma=False,
    )
```

```python
import jax
import jax.numpy as jnp
from jax import lax
from jax.experimental import pallas as pl
from jax.experimental.pallas import tpu as pltpu
from jax.sharding import PartitionSpec as P

MESH = pl.DeviceIdType.MESH
F32 = jnp.float32
BF16 = jnp.bfloat16
NROW, NCOL, NCHAN = 16, 12, 4
ZROWS = 144
COEFS = ((1, 45.0), (2, -9.0), (3, 1.0))
X_COMPS = (0, 3, 4)
Y_COMPS = (3, 1, 5)
Z_COMPS = (4, 5, 2)

NEAR = [(0, dc, dx) for dc in (-1, 0, 1) for dx in (-1, 0, 1) if (dc, dx) != (0, 0)] + [(0, 0, 2)]
BEYOND = [(0, 1, dx) for dx in (-1, 0, 1)]
FAR = [(dr, dc, dx) for dr in (-1, 1) for dc in (-1, 0, 1) for dx in (-1, 0, 1)]


def iota(shape, dim):
    return lax.broadcasted_iota(jnp.int32, shape, dim)


def split(value):
    high = value.astype(BF16)
    return high, (value - high.astype(F32)).astype(BF16)


def split3(value):
    high = value.astype(BF16)
    rest = value - high.astype(F32)
    mid = rest.astype(BF16)
    return high, mid, (rest - mid.astype(F32)).astype(BF16)


def mm(a, b, dims=((1,), (0,)), exact=False):
    return lax.dot_general(
        a,
        b,
        (dims, ((), ())),
        preferred_element_type=F32,
        precision=lax.Precision.HIGHEST if exact else None,
    )


NT = ((1,), (1,))
TN = ((0,), (0,))


def mm2(value, matrix):
    high, low = split(value)
    rows = value.shape[0]
    both = mm(jnp.concatenate([high, low], 0), matrix)
    return both[:rows] + both[rows:]


def stencil_matrix(distance):
    total = jnp.zeros(distance.shape, F32)
    for k, c in COEFS:
        total = jnp.where(distance == k, c, jnp.where(distance == -k, -c, total))
    return total.astype(BF16)


NEAREST, SPARE = (3, 0), (0, 3)


def packed(rows, s):
    high, low = split(rows)
    moved = pltpu.roll(low.astype(F32), (SPARE[s] - NEAREST[s]) % rows.shape[0], 0)
    slot = iota(rows.shape, 0) % 4
    return jnp.where(slot == SPARE[s], moved, high.astype(F32)).astype(BF16)


def unpacked(rows, s):
    rows = rows.astype(F32)
    low = pltpu.roll(rows, (NEAREST[s] - SPARE[s]) % rows.shape[0], 0)
    return rows + jnp.where(iota(rows.shape, 0) % 4 == NEAREST[s], low, 0.0)


def body_kernel(
    vel_in, lift_w_in, lift_b_in, conv_w_in, conv_b_in, head_w_in,
    out, stress_out,
    vel, lift_w, lift_b, conv_w, conv_b, head_w,
    xs, bx, ystage, ydec, ysend, csend, zvsend, yvsend, yvstage, wall,
    yland, cland, xland, zvland, yvland, xv, stx, sland,
    hid, taps, headk, strs, field, edge, base, e2, zd,
    send_sem, recv_sem, load_sem, ready, wrapped,
):
    here = (lax.axis_index("row"), lax.axis_index("col"), lax.axis_index("chan"))
    me = here[2]

    def peer(off):
        return tuple(
            h if o == 0 else lax.rem(h + (o + n) % n, n)
            for h, o, n in zip(here, off, (NROW, NCOL, NCHAN))
        )

    odd = lax.rem(here[0], 2)
    leftmost, rightmost = here[1] == 0, here[1] == NCOL - 1
    barrier = pltpu.get_barrier_semaphore()
    for off in NEAR:
        if off[1] < 1:
            pl.semaphore_signal(barrier, inc=1, device_id=peer(off), device_id_type=MESH)

    @pl.when(jnp.logical_not(rightmost))
    def _():
        for off in BEYOND:
            pl.semaphore_signal(barrier, inc=1, device_id=peer(off), device_id_type=MESH)

    @pl.when(odd == 0)
    def _():
        for off in FAR:
            pl.semaphore_signal(barrier, inc=1, device_id=peer(off), device_id_type=MESH)


    pairs_in = (
        (vel_in, vel), (conv_w_in, conv_w), (lift_w_in, lift_w), (lift_b_in, lift_b),
        (conv_b_in, conv_b), (head_w_in, head_w),
    )
    loads = [
        pltpu.make_async_copy(src, dst, load_sem.at[k]) for k, (src, dst) in enumerate(pairs_in)
    ]
    for load in loads:
        load.start()
    copies = []

    def send(src, dst, source, landed=None, start=True):
        k = len(copies)
        copy = pltpu.make_async_remote_copy(
            src_ref=src, dst_ref=dst, send_sem=send_sem.at[k], recv_sem=recv_sem.at[k],
            device_id=peer(tuple(-s for s in source)), device_id_type=MESH,
        )
        if start:
            copy.start()
        if landed is not None:
            copies.append((copy, pltpu.make_async_remote_copy(
                src_ref=src, dst_ref=landed, send_sem=send_sem.at[k], recv_sem=recv_sem.at[k],
                device_id=peer(tuple(-s for s in source)), device_id_type=MESH,
            )))
        else:
            copies.append((copy, copy))
        return k

    def arrive(ks):
        for k in ks:
            copies[k][1].wait_recv()

    pool = jnp.where(iota((256, 128), 0) // 2 == iota((256, 128), 1), 1.0, 0.0).astype(BF16)
    r16 = iota((16, 256), 0)
    ends = jnp.where(r16 < 4, r16, r16 + 120)
    picker = jnp.where((iota((16, 256), 1) // 2 == ends) & (r16 < 8), 1.0, 0.0).astype(BF16)
    csend[...] = jnp.zeros_like(csend)
    ystage[...] = jnp.zeros_like(ystage)
    loads[0].wait()
    for p in range(2):
        for c in range(3):
            both = vel[2 * p, c] + vel[2 * p + 1, c]
            r = 16 * (3 * p + c)
            xs[0, r : r + 16, :] = both[:, :128]
            xs[1, r : r + 16, :] = both[:, 128:]
    pairs = jnp.concatenate(
        [xs[h, pl.ds(0, 48, 2), :] + xs[h, pl.ds(1, 48, 2), :] for h in range(2)], axis=1
    )
    pieces = split3(pairs * 0.125)
    pooled = mm(jnp.concatenate(pieces, 0), pool)
    box = pooled[0:48] + pooled[48:96] + pooled[96:144]
    bx[0] = box[0:24]
    bx[1] = box[24:48]
    for p in range(2):
        for c in range(3):
            r = 8 * (3 * p + c)
            ystage[0, 16 * p + 4 * c : 16 * p + 4 * c + 4, :] = box[r + 4 : r + 8]
            ystage[1, 16 * p + 4 * c : 16 * p + 4 * c + 4, :] = box[r : r + 4]
    for s in range(2):
        ysend[s] = packed(ystage[s], s).reshape(2, 16, 128)
    columns = mm(picker, pieces[0], NT) + mm(picker, pieces[1], NT) + mm(picker, pieces[2], NT)
    csend[0, :, 0:48] = columns[4:8]
    csend[1, :, 0:48] = columns[0:4]
    for k in range(12):
        yvstage[0, 4 * k : 4 * k + 4, :] = vel[k // 3, k % 3, 12:16, :]
        yvstage[1, 4 * k : 4 * k + 4, :] = vel[k // 3, k % 3, 0:4, :]
    for s in range(2):
        yvsend[s] = packed(yvstage[s], s)

    pl.semaphore_wait(
        barrier, len(NEAR) - jnp.where(leftmost, len(BEYOND), 0) + len(FAR) * odd
    )

    @pl.when(rightmost)
    def _():
        for off in BEYOND:
            pl.semaphore_signal(wrapped, inc=1, device_id=peer(off), device_id_type=MESH)

    ybox, corner, ycols, yvel = [], [], [], []
    for s, dr in ((0, -1), (1, 1)):
        ybox.append(send(ysend.at[s], yland.at[s, 1:3], (dr, 0, 0), start=False))
        ybox.append(send(ysend.at[s, 1], yland.at[s, 0], (dr, 0, -1), start=False))
        ybox.append(send(ysend.at[s, 0], yland.at[s, 3], (dr, 0, 1), start=False))
    for s, dr in ((1, -1), (2, 1)):
        for t, dc in ((0, -1), (1, 1)):
            for dx in (-1, 0, 1):
                corner.append(
                    send(csend.at[t], cland.at[s, t, dx + 1], (dr, dc, dx), start=False)
                )
    for s, dr in ((0, -1), (1, 1)):
        yvel.append(send(yvsend.at[s], yvland.at[s], (dr, 0, 0), start=False))
    far_copies = [copies[k][0] for k in ybox + corner]
    late_copies = [copies[k][0] for k in yvel]

    @pl.when(odd == 1)
    def _():
        for off in FAR:
            pl.semaphore_signal(ready, inc=1, device_id=peer(off), device_id_type=MESH)
        for copy in far_copies:
            copy.start()

    for t, dc in ((0, -1), (1, 1)):
        for dx in (-1, 0, 1):
            ycols.append(
                send(csend.at[t], cland.at[0, t, dx + 1], (0, dc, dx), start=dc == -1)
            )
    left_copies = [copies[k][0] for k in ycols[3:]]

    @pl.when(jnp.logical_not(leftmost))
    def _():
        for copy in left_copies:
            copy.start()

    xbox = [send(bx.at[1], xland.at[0], (0, 0, -1)), send(bx.at[0], xland.at[1], (0, 0, 1))]

    for load in loads[1:]:
        load.wait()
    for k in range(9):
        a, c = k // 3, k % 3
        parts = [conv_w[9 * a + 3 * b + c].astype(F32) for b in range(3)]
        wall[me, 8 * k : 8 * k + 8, :] = jnp.concatenate(parts + [jnp.zeros((8, 32), F32)], axis=1)
    wall[me, 72:80, :] = jnp.zeros((8, 128), F32)
    wall[me, 72:78, 0:8] = head_w[...].astype(F32)
    wall[me, 78:79, 0:8] = conv_b[...].astype(F32)
    weights = [
        send(wall.at[me], wall.at[me], (0, 0, dx), wall.at[lax.rem(me + (dx + 4) % 4, 4)])
        for dx in (-1, 1, 2)
    ]
    rz = iota((16, 256), 0)
    at = jnp.where(rz < 8, rz + 248, rz - 8)
    take = jnp.where(iota((16, 256), 1) == at, 1.0, 0.0)
    zvsend[...] = jnp.zeros_like(zvsend)
    for c in range(3):
        cols = mm(take, vel[:, c].reshape(64, 256), NT, exact=True)
        zvsend[0, c, :, 0:64] = cols[0:8]
        zvsend[1, c, :, 0:64] = cols[8:16]
    zvel = [
        send(zvsend.at[t], zvland.at[t], (0, dc, 0), start=dc == -1) for t, dc in ((0, -1), (1, 1))
    ]

    @pl.when(jnp.logical_not(leftmost))
    def _():
        copies[zvel[1]][0].start()

    xvel = [send(vel.at[1:4], xv.at[0], (0, 0, -1)), send(vel.at[0:3], xv.at[1], (0, 0, 1))]

    spread = jnp.where(iota((32, 256), 1) % 32 == iota((32, 256), 0), 1.0, 0.0)
    bias = mm(lift_b[...], spread, exact=True)
    rows24 = jnp.where(iota((24, 3), 0) // 8 == iota((24, 3), 1), 1.0, 0.0)
    lift = mm(rows24, mm(lift_w[...], spread, exact=True), exact=True)
    lift = jnp.where(iota((24, 256), 0) % 8 == iota((24, 256), 1) // 32, lift, 0.0)
    lift_of = [
        jnp.concatenate([lift, jnp.zeros((104, 256), F32)], 0),
        jnp.concatenate([jnp.zeros((24, 256), F32), lift, jnp.zeros((80, 256), F32)], 0),
    ]

    def hold(q, row, lane, value):
        high, low = split(value)
        n, m = value.shape
        hid[q, row : row + n, lane : lane + m] = high
        hid[q, ZROWS + row : ZROWS + row + n, lane : lane + m] = low

    def lifted(rows):
        return jnp.tanh(mm(rows, lift, TN, exact=True) + bias)

    def side(s, dx):
        return jnp.concatenate(
            [cland[s, 1, dx + 1], jnp.zeros((8, 128), F32), cland[s, 0, dx + 1]], 0
        )

    PLANES = ((0, -1, 1), (1, 0, 0), (2, 0, 1), (3, 1, 0))
    for p in range(2):
        hold(p + 1, 0, 128, lifted(bx[p]))
    arrive(xbox)
    hold(0, 0, 128, lifted(xland[0]))
    hold(3, 0, 128, lifted(xland[1]))

    arrive(weights)
    lane = iota((32, 128), 1)
    zero = jnp.zeros((32, 128), F32)
    for k in range(9):
        a, c = k // 3, k % 3
        x = jnp.concatenate([wall[n, 8 * k : 8 * k + 8, :] for n in range(4)], 0)
        r1, r2, r3 = (pltpu.roll(x, 32 * n, 1) for n in (1, 2, 3))
        tiles = (
            (r1, zero),
            (jnp.where(lane >= 64, r2, 0.0), jnp.where(lane < 64, r2, 0.0)),
            (jnp.where(lane >= 96, r3, 0.0), jnp.where(lane < 96, r3, 0.0)),
            (zero, x),
        )
        for y, (first, second) in enumerate(tiles):
            r = 128 * c + 32 * y
            taps[a, r : r + 32, 0:128] = first.astype(BF16)
            taps[a, r : r + 32, 128:256] = second.astype(BF16)

    @pl.when(odd == 1)
    def _():
        for copy in late_copies:
            copy.start()

    params = wall[0, 72:80, :]
    for n in range(1, 4):
        params = params + pltpu.roll(wall[n, 72:80, :], 8 * n, 1)
    rolled = [params] + [pltpu.roll(params, 32 * n, 1) for n in (1, 2, 3)]
    conv_bias = (rolled[0] + rolled[1] + rolled[2] + rolled[3])[6:7]
    for n in range(4):
        headk[pl.ds(n, 8, 4), :] = rolled[n]
    head = headk[...].astype(BF16)

    @pl.when(leftmost)
    def _():
        pl.semaphore_wait(wrapped, len(BEYOND))
        for copy in left_copies + [copies[zvel[1]][0]]:
            copy.start()

    arrive(ycols)
    for q, dx, p in PLANES:
        hold(q, 128, 128, jnp.tanh(mm(side(0, dx), lift_of[p], exact=True) + bias))

    def closure(g):
        total = None
        for a in range(3):
            block = hid[a : a + 2, :, 128 * g : 128 * g + 256].reshape(4 * ZROWS, 256)
            term = mm(block, taps[a], NT)
            total = term if total is None else total + term
        for p in range(2):
            r = 2 * ZROWS * p
            both = total[r : r + ZROWS] + total[r + ZROWS : r + 2 * ZROWS]
            conv = (
                pltpu.roll(both[:, 0:128], 1, 0)
                + both[:, 128:256]
                + pltpu.roll(both[:, 256:384], ZROWS - 1, 0)
                + conv_bias
            )
            act = 0.5 * conv * (1.0 + jnp.tanh(0.5 * conv))
            high, low = split(act)
            found = mm(head, high, NT) + mm(head, low, NT)
            for s in range(6):
                strs[p, s, 4 * g : 4 * g + 4, 0:ZROWS] = found[4 * s : 4 * s + 4]

    closure(1)

    field[...] = jnp.zeros_like(field)
    for p in range(4):
        uy = vel[p, 1]
        for i in range(3):
            field[p, i, 8:24, :] = uy * vel[p, i]
    stencil = stencil_matrix(iota((256, 256), 0) - iota((256, 256), 1))
    for i in range(3):
        flux = (vel[:, 2] * vel[:, i]).reshape(64, 256)
        base[:, i] = mm2(flux, stencil).reshape(4, 16, 256)
    for p in range(4):
        for i in range(3):
            total = base[p, i]
            for k, c in COEFS:
                total = total + c * (field[p, i, 8 + k : 24 + k, :] - field[p, i, 8 - k : 24 - k, :])
            base[p, i] = total
    arrive(zvel)
    r16z = iota((16, 256), 0)
    place = jnp.where(r16z < 8, r16z - 8, r16z + 248)
    rim = stencil_matrix(place - iota((16, 256), 1)).astype(F32)
    cols = [jnp.concatenate([zvland[0, c], zvland[1, c]], 0)[:, 0:64] for c in range(3)]
    for i in range(3):
        base[:, i] += mm(cols[2] * cols[i], rim, TN, exact=True).reshape(4, 16, 256)
    arrive(xvel)
    for i in range(3):
        planes = (
            [xv[0, n, 0] * xv[0, n, i] for n in range(3)]
            + [vel[n, 0] * vel[n, i] for n in range(4)]
            + [xv[1, n, 0] * xv[1, n, i] for n in range(3)]
        )
        for p in range(4):
            total = base[p, i]
            for k, c in COEFS:
                total = total + c * (planes[p + 3 + k] - planes[p + 3 - k])
            base[p, i] = total

    @pl.when(odd == 0)
    def _():
        pl.semaphore_wait(ready, len(FAR))
        for copy in far_copies:
            copy.start()

    arrive(ybox)

    @pl.when(odd == 0)
    def _():
        for copy in late_copies:
            copy.start()

    for s in range(2):
        ydec[s] = unpacked(yland[s].reshape(64, 128), s)
    for q in range(4):
        rows = jnp.concatenate(
            [ydec[s, 16 * q + 4 * c : 16 * q + 4 * c + 4, :] for c in range(3) for s in (1, 0)], 0
        )
        h = lifted(rows)
        hold(q, 0, 0, h[:, 128:256])
        hold(q, 0, 384, h[:, 0:128])
    arrive(corner)
    for q, dx, p in PLANES:
        rows = jnp.concatenate([side(1, dx), side(2, dx)], 0)
        h = jnp.tanh(mm(rows, lift_of[p], exact=True) + bias)
        hold(q, 128, 0, h[0:16, 128:256])
        hold(q, 128, 384, h[16:32, 0:128])
    closure(0)
    closure(2)

    for p in range(2):
        for i, s in enumerate(X_COMPS):
            stx[p, i] = strs[p, s, 2:10, 0:128]
    xstress = [send(stx, sland.at[0], (0, 0, -1)), send(stx, sland.at[1], (0, 0, 1))]

    for p in range(2):
        for s in range(6):
            stress_out[p, s] = strs[p, s, 2:10, 0:128]

    arrive(yvel)
    edge[...] = jnp.zeros_like(edge)
    above, below = (unpacked(yvland[s], s) for s in range(2))
    for p in range(4):
        for i in range(3):
            k, y, n = 4 * (3 * p + i), 4 * (3 * p + 1), 3 * p + i
            edge[n, 4:8, :] = above[y : y + 4] * above[k : k + 4]
            edge[n, 16:20, :] = below[y : y + 4] * below[k : k + 4]
    for p in range(4):
        for i in range(3):
            n = 3 * p + i
            top = base[p, i, 0:8]
            bottom = base[p, i, 8:16]
            for k, c in COEFS:
                top = top - c * edge[n, 8 - k : 16 - k, :]
                bottom = bottom + c * edge[n, 8 + k : 16 + k, :]
            base[p, i, 0:8] = top
            base[p, i, 8:16] = bottom

    l144, c256 = iota((ZROWS, 256), 0), iota((ZROWS, 256), 1)
    dist = jnp.where(l144 < 136, l144, l144 - ZROWS) - c256 // 2
    even = jnp.where(dist == 0, 45.0, jnp.where(dist == -1, -36.0, jnp.where(dist == 1, -8.0, jnp.where(dist == -2, -1.0, 0.0))))
    odd = jnp.where(dist == 1, 36.0, jnp.where(dist == 0, -45.0, jnp.where(dist == -1, 8.0, jnp.where(dist == 2, 1.0, 0.0))))
    along = jnp.where(c256 % 2 == 0, even, odd).astype(BF16)
    zrows = jnp.concatenate(
        [strs[p, s, 2:10, 0:ZROWS] for p in range(2) for s in Z_COMPS], 0
    )
    zder = mm2(zrows, along)
    for p in range(2):
        for i in range(3):
            r = 8 * (3 * p + i)
            for half in range(2):
                piece = zder[r : r + 8, 128 * half : 128 * half + 128]
                zd[p, i, half, pl.ds(0, 8, 2), :] = piece
                zd[p, i, half, pl.ds(1, 8, 2), :] = piece
    yder = []
    for p in range(2):
        for i, s in enumerate(Y_COMPS):
            c = {k: strs[p, s, 2 + k : 10 + k, 0:128] for k in range(-2, 3)}
            yder.append((
                45.0 * c[0] - 36.0 * c[-1] - 8.0 * c[1] - c[-2],
                36.0 * c[1] - 45.0 * c[0] + 8.0 * c[-1] + c[2],
            ))
    double = jnp.where(iota((128, 256), 1) // 2 == iota((128, 256), 0), 1.0, 0.0).astype(BF16)

    arrive(xstress)
    for i in range(3):
        c = [sland[0, 0, i], sland[0, 1, i], stx[0, i], stx[1, i], sland[1, 0, i], sland[1, 1, i]]
        for p in range(2):
            n = p + 2
            xder = (
                45.0 * c[n] - 36.0 * c[n - 1] - 8.0 * c[n + 1] - c[n - 2],
                36.0 * c[n + 1] - 45.0 * c[n] + 8.0 * c[n - 1] + c[n + 2],
            )
            for px in range(2):
                for py in range(2):
                    e2[2 * p + px, i, pl.ds(py, 8, 2), :] = xder[px] + yder[3 * p + i][py]
    fine = mm2(e2[...].reshape(192, 128), double)
    for p in range(4):
        for i in range(3):
            r = 16 * (3 * p + i)
            zpart = jnp.concatenate([zd[p // 2, i, 0], zd[p // 2, i, 1]], axis=1)
            total = base[p, i] + fine[r : r + 16] + zpart
            out[p, i] = vel[p, i] - (0.1 / 60.0) * total

    for copy, _ in copies:
        copy.wait_send()


def body(velocity, lift_weight, lift_bias, conv_weight, conv_bias, head_weight):
    vmem = pl.BlockSpec(memory_space=pltpu.VMEM)
    ncopies = 6 + 12 + 6 + 2 + 2 + 3 + 2 + 2 + 2
    scratch = [
        pltpu.VMEM((4, 3, 16, 256), F32),
        pltpu.VMEM((3, 32), F32),
        pltpu.VMEM((1, 32), F32),
        pltpu.VMEM((27, 8, 32), BF16),
        pltpu.VMEM((1, 8), BF16),
        pltpu.VMEM((6, 8), BF16),
        pltpu.VMEM((2, 96, 128), F32),
        pltpu.VMEM((2, 24, 128), F32),
        pltpu.VMEM((2, 32, 128), F32),
        pltpu.VMEM((2, 64, 128), F32),
        pltpu.VMEM((2, 2, 16, 128), BF16),
        pltpu.VMEM((2, 4, 128), F32),
        pltpu.VMEM((2, 3, 8, 128), F32),
        pltpu.VMEM((2, 48, 256), BF16),
        pltpu.VMEM((2, 48, 256), F32),
        pltpu.VMEM((4, 80, 128), F32),
        pltpu.VMEM((2, 4, 16, 128), BF16),
        pltpu.VMEM((3, 2, 3, 4, 128), F32),
        pltpu.VMEM((2, 24, 128), F32),
        pltpu.VMEM((2, 3, 8, 128), F32),
        pltpu.VMEM((2, 48, 256), BF16),
        pltpu.VMEM((2, 3, 3, 16, 256), F32),
        pltpu.VMEM((2, 3, 8, 128), F32),
        pltpu.VMEM((2, 2, 3, 8, 128), F32),
        pltpu.VMEM((4, 2 * ZROWS, 512), BF16),
        pltpu.VMEM((3, 384, 256), BF16),
        pltpu.VMEM((32, 128), F32),
        pltpu.VMEM((2, 6, 16, 256), F32),
        pltpu.VMEM((4, 3, 32, 256), F32),
        pltpu.VMEM((12, 24, 256), F32),
        pltpu.VMEM((4, 3, 16, 256), F32),
        pltpu.VMEM((4, 3, 16, 128), F32),
        pltpu.VMEM((2, 3, 2, 16, 128), F32),
        pltpu.SemaphoreType.DMA((ncopies,)),
        pltpu.SemaphoreType.DMA((ncopies,)),
        pltpu.SemaphoreType.DMA((6,)),
        pltpu.SemaphoreType.REGULAR,
        pltpu.SemaphoreType.REGULAR,
    ]
    return pl.pallas_call(
        body_kernel,
        out_shape=(
            pltpu.VMEM((4, 3, 16, 256), F32),
            pltpu.VMEM((2, 6, 8, 128), F32),
        ),
        in_specs=[pl.BlockSpec(memory_space=pltpu.HBM)] * 6,
        out_specs=(vmem, vmem),
        scratch_shapes=scratch,
        compiler_params=pltpu.CompilerParams(
            collective_id=0, has_side_effects=True, vmem_limit_bytes=60 * 2**20
        ),
    )(
        velocity,
        lift_weight.T,
        lift_bias.reshape(1, 32),
        conv_weight,
        conv_bias.reshape(1, 8),
        head_weight,
    )


def solution(mesh):
    placed = (
        P("chan", None, "row", "col"),
        P(),
        P(),
        P(None, "chan", None),
        P("chan"),
        P(None, "chan"),
    )
    return jax.shard_map(
        body,
        mesh=mesh,
        in_specs=placed,
        out_specs=(P("chan", None, "row", "col"), P("chan", None, "row", "col")),
        check_vma=False,
    )
```

```python
import jax
import jax.numpy as jnp
from jax import lax
from jax.experimental import pallas as pl
from jax.experimental.pallas import tpu as pltpu
from jax.sharding import PartitionSpec as P

MESH = pl.DeviceIdType.MESH
F32 = jnp.float32
BF16 = jnp.bfloat16
NROW, NCOL, NCHAN = 16, 12, 4
ZROWS = 144
COEFS = ((1, 45.0), (2, -9.0), (3, 1.0))
X_COMPS = (0, 3, 4)
Y_COMPS = (3, 1, 5)
Z_COMPS = (4, 5, 2)

NEAR = [(0, dc, dx) for dc in (-1, 0, 1) for dx in (-1, 0, 1) if (dc, dx) != (0, 0)] + [(0, 0, 2)]
BEYOND = [(0, 1, dx) for dx in (-1, 0, 1)]
FAR = [(dr, dc, dx) for dr in (-1, 1) for dc in (-1, 0, 1) for dx in (-1, 0, 1)]


def iota(shape, dim):
    return lax.broadcasted_iota(jnp.int32, shape, dim)


def split(value):
    high = value.astype(BF16)
    return high, (value - high.astype(F32)).astype(BF16)


def split3(value):
    high = value.astype(BF16)
    rest = value - high.astype(F32)
    mid = rest.astype(BF16)
    return high, mid, (rest - mid.astype(F32)).astype(BF16)


def mm(a, b, dims=((1,), (0,)), exact=False):
    return lax.dot_general(
        a,
        b,
        (dims, ((), ())),
        preferred_element_type=F32,
        precision=lax.Precision.HIGHEST if exact else None,
    )


NT = ((1,), (1,))
TN = ((0,), (0,))


def mm2(value, matrix):
    high, low = split(value)
    rows = value.shape[0]
    both = mm(jnp.concatenate([high, low], 0), matrix)
    return both[:rows] + both[rows:]


def stencil_matrix(distance):
    total = jnp.zeros(distance.shape, F32)
    for k, c in COEFS:
        total = jnp.where(distance == k, c, jnp.where(distance == -k, -c, total))
    return total.astype(BF16)


NEAREST, SPARE = (3, 0), (0, 3)


def packed(rows, s):
    high, low = split(rows)
    moved = pltpu.roll(low.astype(F32), (SPARE[s] - NEAREST[s]) % rows.shape[0], 0)
    slot = iota(rows.shape, 0) % 4
    return jnp.where(slot == SPARE[s], moved, high.astype(F32)).astype(BF16)


def unpacked(rows, s):
    rows = rows.astype(F32)
    low = pltpu.roll(rows, (NEAREST[s] - SPARE[s]) % rows.shape[0], 0)
    return rows + jnp.where(iota(rows.shape, 0) % 4 == NEAREST[s], low, 0.0)


def skewed(rows, start, step):
    turn = iota(rows.shape, 0) % 4
    total = pltpu.roll(rows, start % 128, 1) if start % 128 else rows
    for n in range(1, 4):
        total = jnp.where(turn == n, pltpu.roll(rows, (start + step * n) % 128, 1), total)
    return total


def body_kernel(
    vel_in, lift_w_in, lift_b_in, conv_w_in, conv_b_in, head_w_in,
    out, stress_out,
    vel, lift_w, lift_b, conv_w, conv_b, head_w,
    xs, bx, ystage, ydec, ysend, csend, zvsend, yvsend, yvstage, wall,
    yland, cland, cpack, cfar, cwide, xland, zvland, yvland, xv, stx, sland,
    hid, taps, early, headk, strs, field, edge, base, e2, zd,
    send_sem, recv_sem, load_sem, ready, wrapped,
):
    here = (lax.axis_index("row"), lax.axis_index("col"), lax.axis_index("chan"))
    me = here[2]

    def peer(off):
        return tuple(
            h if o == 0 else lax.rem(h + (o + n) % n, n)
            for h, o, n in zip(here, off, (NROW, NCOL, NCHAN))
        )

    odd = lax.rem(here[0], 2)
    leftmost, rightmost = here[1] == 0, here[1] == NCOL - 1
    barrier = pltpu.get_barrier_semaphore()
    for off in NEAR:
        if off[1] < 1:
            pl.semaphore_signal(barrier, inc=1, device_id=peer(off), device_id_type=MESH)

    @pl.when(jnp.logical_not(rightmost))
    def _():
        for off in BEYOND:
            pl.semaphore_signal(barrier, inc=1, device_id=peer(off), device_id_type=MESH)

    @pl.when(odd == 0)
    def _():
        for off in FAR:
            pl.semaphore_signal(barrier, inc=1, device_id=peer(off), device_id_type=MESH)


    pairs_in = (
        (vel_in, vel), (conv_w_in, conv_w), (lift_w_in, lift_w), (lift_b_in, lift_b),
        (conv_b_in, conv_b), (head_w_in, head_w),
    )
    loads = [
        pltpu.make_async_copy(src, dst, load_sem.at[k]) for k, (src, dst) in enumerate(pairs_in)
    ]
    for load in loads:
        load.start()
    copies = []

    def send(src, dst, source, landed=None, start=True):
        k = len(copies)
        copy = pltpu.make_async_remote_copy(
            src_ref=src, dst_ref=dst, send_sem=send_sem.at[k], recv_sem=recv_sem.at[k],
            device_id=peer(tuple(-s for s in source)), device_id_type=MESH,
        )
        if start:
            copy.start()
        if landed is not None:
            copies.append((copy, pltpu.make_async_remote_copy(
                src_ref=src, dst_ref=landed, send_sem=send_sem.at[k], recv_sem=recv_sem.at[k],
                device_id=peer(tuple(-s for s in source)), device_id_type=MESH,
            )))
        else:
            copies.append((copy, copy))
        return k

    def arrive(ks):
        for k in ks:
            copies[k][1].wait_recv()

    pool = jnp.where(iota((256, 128), 0) // 2 == iota((256, 128), 1), 1.0, 0.0).astype(BF16)
    r16 = iota((16, 256), 0)
    ends = jnp.where(r16 < 4, r16, r16 + 120)
    picker = jnp.where((iota((16, 256), 1) // 2 == ends) & (r16 < 8), 1.0, 0.0).astype(BF16)
    csend[...] = jnp.zeros_like(csend)
    ystage[...] = jnp.zeros_like(ystage)
    loads[0].wait()
    for p in range(2):
        for c in range(3):
            both = vel[2 * p, c] + vel[2 * p + 1, c]
            r = 16 * (3 * p + c)
            xs[0, r : r + 16, :] = both[:, :128]
            xs[1, r : r + 16, :] = both[:, 128:]
    pairs = jnp.concatenate(
        [xs[h, pl.ds(0, 48, 2), :] + xs[h, pl.ds(1, 48, 2), :] for h in range(2)], axis=1
    )
    pieces = split3(pairs * 0.125)
    pooled = mm(jnp.concatenate(pieces, 0), pool)
    box = pooled[0:48] + pooled[48:96] + pooled[96:144]
    bx[0] = box[0:24]
    bx[1] = box[24:48]
    for p in range(2):
        for c in range(3):
            r = 8 * (3 * p + c)
            ystage[0, 16 * p + 4 * c : 16 * p + 4 * c + 4, :] = box[r + 4 : r + 8]
            ystage[1, 16 * p + 4 * c : 16 * p + 4 * c + 4, :] = box[r : r + 4]
    for s in range(2):
        ysend[s] = packed(ystage[s], s).reshape(2, 16, 128)
    columns = mm(picker, pieces[0], NT) + mm(picker, pieces[1], NT) + mm(picker, pieces[2], NT)
    csend[0, :, 0:48] = columns[4:8]
    csend[1, :, 0:48] = columns[0:4]
    ends8 = csend[...].reshape(8, 128)
    lane8 = iota((8, 128), 1)
    for p in range(2):
        mine = jnp.where((lane8 >= 24 * p) & (lane8 < 24 * p + 24), ends8, 0.0)
        spaced = skewed(mine, 128 - 24 * p, 32)
        for t in range(2):
            row = spaced[4 * t : 4 * t + 1]
            for n in range(1, 4):
                row = row + spaced[4 * t + n : 4 * t + n + 1]
            cpack[t, p] = row
    cwide[...] = jnp.zeros_like(cwide)
    for k in range(12):
        yvstage[0, 4 * k : 4 * k + 4, :] = vel[k // 3, k % 3, 12:16, :]
        yvstage[1, 4 * k : 4 * k + 4, :] = vel[k // 3, k % 3, 0:4, :]
    for s in range(2):
        yvsend[s] = packed(yvstage[s], s)

    pl.semaphore_wait(
        barrier, len(NEAR) - jnp.where(leftmost, len(BEYOND), 0) + len(FAR) * odd
    )

    @pl.when(rightmost)
    def _():
        for off in BEYOND:
            pl.semaphore_signal(wrapped, inc=1, device_id=peer(off), device_id_type=MESH)

    ybox, corner, ycols, yvel = [], [], [], []
    for s, dr in ((0, -1), (1, 1)):
        ybox.append(send(ysend.at[s], yland.at[s, 1:3], (dr, 0, 0), start=False))
        ybox.append(send(ysend.at[s, 1], yland.at[s, 0], (dr, 0, -1), start=False))
        ybox.append(send(ysend.at[s, 0], yland.at[s, 3], (dr, 0, 1), start=False))
    for s, dr in ((0, -1), (1, 1)):
        for t, dc in ((0, -1), (1, 1)):
            corner += [
                send(cpack.at[t, 1], cfar.at[s, t, 0], (dr, dc, -1), start=False),
                send(cpack.at[t], cfar.at[s, t, 1:3], (dr, dc, 0), start=False),
                send(cpack.at[t, 0], cfar.at[s, t, 3], (dr, dc, 1), start=False),
            ]
    for s, dr in ((0, -1), (1, 1)):
        yvel.append(send(yvsend.at[s], yvland.at[s], (dr, 0, 0), start=False))
    far_copies = [copies[k][0] for k in ybox + corner]
    late_copies = [copies[k][0] for k in yvel]

    @pl.when(odd == 1)
    def _():
        for off in FAR:
            pl.semaphore_signal(ready, inc=1, device_id=peer(off), device_id_type=MESH)
        for copy in far_copies:
            copy.start()

    for t, dc in ((0, -1), (1, 1)):
        for dx in (-1, 0, 1):
            ycols.append(
                send(csend.at[t], cland.at[t, dx + 1], (0, dc, dx), start=dc == -1)
            )
    left_copies = [copies[k][0] for k in ycols[3:]]

    @pl.when(jnp.logical_not(leftmost))
    def _():
        for copy in left_copies:
            copy.start()

    xbox = [send(bx.at[1], xland.at[0], (0, 0, -1)), send(bx.at[0], xland.at[1], (0, 0, 1))]

    for load in loads[1:]:
        load.wait()
    for k in range(9):
        a, c = k // 3, k % 3
        parts = [conv_w[9 * a + 3 * b + c].astype(F32) for b in range(3)]
        wall[me, 8 * k : 8 * k + 8, :] = jnp.concatenate(parts + [jnp.zeros((8, 32), F32)], axis=1)
    wall[me, 72:80, :] = jnp.zeros((8, 128), F32)
    wall[me, 72:78, 0:8] = head_w[...].astype(F32)
    wall[me, 78:79, 0:8] = conv_b[...].astype(F32)
    weights = [
        send(wall.at[me], wall.at[me], (0, 0, dx), wall.at[lax.rem(me + (dx + 4) % 4, 4)])
        for dx in (-1, 1, 2)
    ]
    rz = iota((16, 256), 0)
    at = jnp.where(rz < 8, rz + 248, rz - 8)
    take = jnp.where(iota((16, 256), 1) == at, 1.0, 0.0)
    zvsend[...] = jnp.zeros_like(zvsend)
    for c in range(3):
        cols = mm(take, vel[:, c].reshape(64, 256), NT, exact=True)
        zvsend[0, c, :, 0:64] = cols[0:8]
        zvsend[1, c, :, 0:64] = cols[8:16]
    zvel = [
        send(zvsend.at[t], zvland.at[t], (0, dc, 0), start=dc == -1) for t, dc in ((0, -1), (1, 1))
    ]

    @pl.when(jnp.logical_not(leftmost))
    def _():
        copies[zvel[1]][0].start()

    xvel = [send(vel.at[1:4], xv.at[0], (0, 0, -1)), send(vel.at[0:3], xv.at[1], (0, 0, 1))]

    spread = jnp.where(iota((32, 256), 1) % 32 == iota((32, 256), 0), 1.0, 0.0)
    bias = mm(lift_b[...], spread, exact=True)
    rows24 = jnp.where(iota((24, 3), 0) // 8 == iota((24, 3), 1), 1.0, 0.0)
    lift = mm(rows24, mm(lift_w[...], spread, exact=True), exact=True)
    lift = jnp.where(iota((24, 256), 0) % 8 == iota((24, 256), 1) // 32, lift, 0.0)
    lift_of = [
        jnp.concatenate([lift, jnp.zeros((104, 256), F32)], 0),
        jnp.concatenate([jnp.zeros((24, 256), F32), lift, jnp.zeros((80, 256), F32)], 0),
    ]

    def hold(q, row, lane, value):
        high, low = split(value)
        n, m = value.shape
        hid[q, row : row + n, lane : lane + m] = high
        hid[q, ZROWS + row : ZROWS + row + n, lane : lane + m] = low

    def lifted(rows):
        return jnp.tanh(mm(rows, lift, TN, exact=True) + bias)

    def side(dx):
        return jnp.concatenate(
            [cland[1, dx + 1], jnp.zeros((8, 128), F32), cland[0, dx + 1]], 0
        )

    PLANES = ((0, -1, 1), (1, 0, 0), (2, 0, 1), (3, 1, 0))
    for p in range(2):
        hold(p + 1, 0, 128, lifted(bx[p]))
    arrive(xbox)
    hold(0, 0, 128, lifted(xland[0]))
    hold(3, 0, 128, lifted(xland[1]))

    arrive(weights)
    lane = iota((32, 128), 1)
    zero = jnp.zeros((32, 128), F32)
    for k in range(9):
        a, c = k // 3, k % 3
        x = jnp.concatenate([wall[n, 8 * k : 8 * k + 8, :] for n in range(4)], 0)
        r1, r2, r3 = (pltpu.roll(x, 32 * n, 1) for n in (1, 2, 3))
        tiles = (
            (r1, zero),
            (jnp.where(lane >= 64, r2, 0.0), jnp.where(lane < 64, r2, 0.0)),
            (jnp.where(lane >= 96, r3, 0.0), jnp.where(lane < 96, r3, 0.0)),
            (zero, x),
        )
        for y, (first, second) in enumerate(tiles):
            r = 128 * c + 32 * y
            for h, half in enumerate((first, second)):
                taps[h, a, r : r + 32, 0:128] = half.astype(BF16)
                taps[h, a, r : r + 32, 128:256] = half.astype(BF16)

    @pl.when(odd == 1)
    def _():
        for copy in late_copies:
            copy.start()

    params = wall[0, 72:80, :]
    for n in range(1, 4):
        params = params + pltpu.roll(wall[n, 72:80, :], 8 * n, 1)
    rolled = [params] + [pltpu.roll(params, 32 * n, 1) for n in (1, 2, 3)]
    conv_bias = (rolled[0] + rolled[1] + rolled[2] + rolled[3])[6:7]
    for n in range(4):
        headk[pl.ds(n, 8, 4), :] = rolled[n]
    head = headk[...].astype(BF16)

    @pl.when(leftmost)
    def _():
        pl.semaphore_wait(wrapped, len(BEYOND))
        for copy in left_copies + [copies[zvel[1]][0]]:
            copy.start()

    arrive(ycols)
    for q, dx, p in PLANES:
        hold(q, 128, 128, jnp.tanh(mm(side(dx), lift_of[p], exact=True) + bias))

    def partial(h, tile):
        total = None
        for a in range(3):
            block = [hid[a : a + 2, n : n + ZROWS, 128 * tile : 128 * tile + 128] for n in (0, ZROWS)]
            block = jnp.concatenate(block, axis=2).reshape(2 * ZROWS, 256)
            term = mm(block, taps[h, a], NT)
            total = term if total is None else total + term
        return total

    def closure(g, total):
        for p in range(2):
            both = total[ZROWS * p : ZROWS * p + ZROWS]
            conv = (
                pltpu.roll(both[:, 0:128], 1, 0)
                + both[:, 128:256]
                + pltpu.roll(both[:, 256:384], ZROWS - 1, 0)
                + conv_bias
            )
            act = 0.5 * conv * (1.0 + jnp.tanh(0.5 * conv))
            high, low = split(act)
            found = mm(head, high, NT) + mm(head, low, NT)
            for s in range(6):
                strs[p, s, 4 * g : 4 * g + 4, 0:ZROWS] = found[4 * s : 4 * s + 4]

    closure(1, partial(0, 1) + partial(1, 2))
    early[0] = partial(1, 1)
    early[1] = partial(0, 2)

    field[...] = jnp.zeros_like(field)
    for p in range(4):
        uy = vel[p, 1]
        for i in range(3):
            field[p, i, 8:24, :] = uy * vel[p, i]
    stencil = stencil_matrix(iota((256, 256), 0) - iota((256, 256), 1))
    for i in range(3):
        flux = (vel[:, 2] * vel[:, i]).reshape(64, 256)
        base[:, i] = mm2(flux, stencil).reshape(4, 16, 256)
    for p in range(4):
        for i in range(3):
            total = base[p, i]
            for k, c in COEFS:
                total = total + c * (field[p, i, 8 + k : 24 + k, :] - field[p, i, 8 - k : 24 - k, :])
            base[p, i] = total
    arrive(zvel)
    r16z = iota((16, 256), 0)
    place = jnp.where(r16z < 8, r16z - 8, r16z + 248)
    rim = stencil_matrix(place - iota((16, 256), 1)).astype(F32)
    cols = [jnp.concatenate([zvland[0, c], zvland[1, c]], 0)[:, 0:64] for c in range(3)]
    for i in range(3):
        base[:, i] += mm(cols[2] * cols[i], rim, TN, exact=True).reshape(4, 16, 256)
    arrive(xvel)
    for i in range(3):
        planes = (
            [xv[0, n, 0] * xv[0, n, i] for n in range(3)]
            + [vel[n, 0] * vel[n, i] for n in range(4)]
            + [xv[1, n, 0] * xv[1, n, i] for n in range(3)]
        )
        for p in range(4):
            total = base[p, i]
            for k, c in COEFS:
                total = total + c * (planes[p + 3 + k] - planes[p + 3 - k])
            base[p, i] = total

    @pl.when(odd == 0)
    def _():
        pl.semaphore_wait(ready, len(FAR))
        for copy in far_copies:
            copy.start()

    arrive(ybox)

    @pl.when(odd == 0)
    def _():
        for copy in late_copies:
            copy.start()

    for s in range(2):
        ydec[s] = unpacked(yland[s].reshape(64, 128), s)
    for q in range(4):
        rows = jnp.concatenate(
            [ydec[s, 16 * q + 4 * c : 16 * q + 4 * c + 4, :] for c in range(3) for s in (1, 0)], 0
        )
        h = lifted(rows)
        hold(q, 0, 0, h[:, 128:256])
        hold(q, 0, 384, h[:, 0:128])
    arrive(corner)
    for q in range(4):
        for s in range(2):
            r = 16 * (2 * q + s)
            cwide[r : r + 4, :] = jnp.broadcast_to(cfar[s, 1, q], (4, 128))
            cwide[r + 12 : r + 16, :] = jnp.broadcast_to(cfar[s, 0, q], (4, 128))
    rows = skewed(cwide[...], 128, 96)
    h = jnp.tanh(mm(rows, lift_of[0], exact=True) + bias)
    for q in range(4):
        hold(q, 128, 0, h[32 * q : 32 * q + 16, 128:256])
        hold(q, 128, 384, h[32 * q + 16 : 32 * q + 32, 0:128])
    closure(0, early[0] + partial(0, 0))
    closure(2, early[1] + partial(1, 3))

    for p in range(2):
        for i, s in enumerate(X_COMPS):
            stx[p, i] = strs[p, s, 2:10, 0:128]
    xstress = [send(stx, sland.at[0], (0, 0, -1)), send(stx, sland.at[1], (0, 0, 1))]

    for p in range(2):
        for s in range(6):
            stress_out[p, s] = strs[p, s, 2:10, 0:128]

    arrive(yvel)
    edge[...] = jnp.zeros_like(edge)
    above, below = (unpacked(yvland[s], s) for s in range(2))
    for p in range(4):
        for i in range(3):
            k, y, n = 4 * (3 * p + i), 4 * (3 * p + 1), 3 * p + i
            edge[n, 4:8, :] = above[y : y + 4] * above[k : k + 4]
            edge[n, 16:20, :] = below[y : y + 4] * below[k : k + 4]
    for p in range(4):
        for i in range(3):
            n = 3 * p + i
            top = base[p, i, 0:8]
            bottom = base[p, i, 8:16]
            for k, c in COEFS:
                top = top - c * edge[n, 8 - k : 16 - k, :]
                bottom = bottom + c * edge[n, 8 + k : 16 + k, :]
            base[p, i, 0:8] = top
            base[p, i, 8:16] = bottom

    l144, c256 = iota((ZROWS, 256), 0), iota((ZROWS, 256), 1)
    dist = jnp.where(l144 < 136, l144, l144 - ZROWS) - c256 // 2
    even = jnp.where(dist == 0, 45.0, jnp.where(dist == -1, -36.0, jnp.where(dist == 1, -8.0, jnp.where(dist == -2, -1.0, 0.0))))
    odd = jnp.where(dist == 1, 36.0, jnp.where(dist == 0, -45.0, jnp.where(dist == -1, 8.0, jnp.where(dist == 2, 1.0, 0.0))))
    along = jnp.where(c256 % 2 == 0, even, odd).astype(BF16)
    zrows = jnp.concatenate(
        [strs[p, s, 2:10, 0:ZROWS] for p in range(2) for s in Z_COMPS], 0
    )
    zder = mm2(zrows, along)
    for p in range(2):
        for i in range(3):
            r = 8 * (3 * p + i)
            for half in range(2):
                piece = zder[r : r + 8, 128 * half : 128 * half + 128]
                zd[p, i, half, pl.ds(0, 8, 2), :] = piece
                zd[p, i, half, pl.ds(1, 8, 2), :] = piece
    yder = []
    for p in range(2):
        for i, s in enumerate(Y_COMPS):
            c = {k: strs[p, s, 2 + k : 10 + k, 0:128] for k in range(-2, 3)}
            yder.append((
                45.0 * c[0] - 36.0 * c[-1] - 8.0 * c[1] - c[-2],
                36.0 * c[1] - 45.0 * c[0] + 8.0 * c[-1] + c[2],
            ))
    double = jnp.where(iota((128, 256), 1) // 2 == iota((128, 256), 0), 1.0, 0.0).astype(BF16)

    arrive(xstress)
    for i in range(3):
        c = [sland[0, 0, i], sland[0, 1, i], stx[0, i], stx[1, i], sland[1, 0, i], sland[1, 1, i]]
        for p in range(2):
            n = p + 2
            xder = (
                45.0 * c[n] - 36.0 * c[n - 1] - 8.0 * c[n + 1] - c[n - 2],
                36.0 * c[n + 1] - 45.0 * c[n] + 8.0 * c[n - 1] + c[n + 2],
            )
            for px in range(2):
                for py in range(2):
                    e2[2 * p + px, i, pl.ds(py, 8, 2), :] = xder[px] + yder[3 * p + i][py]
    fine = mm2(e2[...].reshape(192, 128), double)
    for p in range(4):
        for i in range(3):
            r = 16 * (3 * p + i)
            zpart = jnp.concatenate([zd[p // 2, i, 0], zd[p // 2, i, 1]], axis=1)
            total = base[p, i] + fine[r : r + 16] + zpart
            out[p, i] = vel[p, i] - (0.1 / 60.0) * total

    for copy, _ in copies:
        copy.wait_send()


def body(velocity, lift_weight, lift_bias, conv_weight, conv_bias, head_weight):
    vmem = pl.BlockSpec(memory_space=pltpu.VMEM)
    ncopies = 6 + 12 + 6 + 2 + 2 + 3 + 2 + 2 + 2
    scratch = [
        pltpu.VMEM((4, 3, 16, 256), F32),
        pltpu.VMEM((3, 32), F32),
        pltpu.VMEM((1, 32), F32),
        pltpu.VMEM((27, 8, 32), BF16),
        pltpu.VMEM((1, 8), BF16),
        pltpu.VMEM((6, 8), BF16),
        pltpu.VMEM((2, 96, 128), F32),
        pltpu.VMEM((2, 24, 128), F32),
        pltpu.VMEM((2, 32, 128), F32),
        pltpu.VMEM((2, 64, 128), F32),
        pltpu.VMEM((2, 2, 16, 128), BF16),
        pltpu.VMEM((2, 4, 128), F32),
        pltpu.VMEM((2, 3, 8, 128), F32),
        pltpu.VMEM((2, 48, 256), BF16),
        pltpu.VMEM((2, 48, 256), F32),
        pltpu.VMEM((4, 80, 128), F32),
        pltpu.VMEM((2, 4, 16, 128), BF16),
        pltpu.VMEM((2, 3, 4, 128), F32),
        pltpu.VMEM((2, 2, 1, 128), F32),
        pltpu.VMEM((2, 2, 4, 1, 128), F32),
        pltpu.VMEM((128, 128), F32),
        pltpu.VMEM((2, 24, 128), F32),
        pltpu.VMEM((2, 3, 8, 128), F32),
        pltpu.VMEM((2, 48, 256), BF16),
        pltpu.VMEM((2, 3, 3, 16, 256), F32),
        pltpu.VMEM((2, 3, 8, 128), F32),
        pltpu.VMEM((2, 2, 3, 8, 128), F32),
        pltpu.VMEM((4, 2 * ZROWS, 512), BF16),
        pltpu.VMEM((2, 3, 384, 256), BF16),
        pltpu.VMEM((2, 2 * ZROWS, 384), F32),
        pltpu.VMEM((32, 128), F32),
        pltpu.VMEM((2, 6, 16, 256), F32),
        pltpu.VMEM((4, 3, 32, 256), F32),
        pltpu.VMEM((12, 24, 256), F32),
        pltpu.VMEM((4, 3, 16, 256), F32),
        pltpu.VMEM((4, 3, 16, 128), F32),
        pltpu.VMEM((2, 3, 2, 16, 128), F32),
        pltpu.SemaphoreType.DMA((ncopies,)),
        pltpu.SemaphoreType.DMA((ncopies,)),
        pltpu.SemaphoreType.DMA((6,)),
        pltpu.SemaphoreType.REGULAR,
        pltpu.SemaphoreType.REGULAR,
    ]
    return pl.pallas_call(
        body_kernel,
        out_shape=(
            pltpu.VMEM((4, 3, 16, 256), F32),
            pltpu.VMEM((2, 6, 8, 128), F32),
        ),
        in_specs=[pl.BlockSpec(memory_space=pltpu.HBM)] * 6,
        out_specs=(vmem, vmem),
        scratch_shapes=scratch,
        compiler_params=pltpu.CompilerParams(
            collective_id=0, has_side_effects=True, vmem_limit_bytes=60 * 2**20
        ),
    )(
        velocity,
        lift_weight.T,
        lift_bias.reshape(1, 32),
        conv_weight,
        conv_bias.reshape(1, 8),
        head_weight,
    )


def solution(mesh):
    placed = (
        P("chan", None, "row", "col"),
        P(),
        P(),
        P(None, "chan", None),
        P("chan"),
        P(None, "chan"),
    )
    return jax.shard_map(
        body,
        mesh=mesh,
        in_specs=placed,
        out_specs=(P("chan", None, "row", "col"), P("chan", None, "row", "col")),
        check_vma=False,
    )
```

```python
import jax
import jax.numpy as jnp
from jax import lax
from jax.experimental import pallas as pl
from jax.experimental.pallas import tpu as pltpu
from jax.sharding import PartitionSpec as P

MESH = pl.DeviceIdType.MESH
F32 = jnp.float32
BF16 = jnp.bfloat16
NROW, NCOL, NCHAN = 16, 12, 4
ZROWS = 144
COEFS = ((1, 45.0), (2, -9.0), (3, 1.0))
X_COMPS = (0, 3, 4)
Y_COMPS = (3, 1, 5)
Z_COMPS = (4, 5, 2)

NEAR = [(0, dc, dx) for dc in (-1, 0, 1) for dx in (-1, 0, 1) if (dc, dx) != (0, 0)] + [(0, 0, 2)]
BEYOND = [(0, 1, dx) for dx in (-1, 0, 1)]
FAR = [(dr, dc, dx) for dr in (-1, 1) for dc in (-1, 0, 1) for dx in (-1, 0, 1)]


def iota(shape, dim):
    return lax.broadcasted_iota(jnp.int32, shape, dim)


def split(value):
    high = value.astype(BF16)
    return high, (value - high.astype(F32)).astype(BF16)


def split3(value):
    high = value.astype(BF16)
    rest = value - high.astype(F32)
    mid = rest.astype(BF16)
    return high, mid, (rest - mid.astype(F32)).astype(BF16)


def mm(a, b, dims=((1,), (0,)), exact=False):
    return lax.dot_general(
        a,
        b,
        (dims, ((), ())),
        preferred_element_type=F32,
        precision=lax.Precision.HIGHEST if exact else None,
    )


NT = ((1,), (1,))
TN = ((0,), (0,))


def mm2(value, matrix):
    high, low = split(value)
    rows = value.shape[0]
    both = mm(jnp.concatenate([high, low], 0), matrix)
    return both[:rows] + both[rows:]


def stencil_matrix(distance):
    total = jnp.zeros(distance.shape, F32)
    for k, c in COEFS:
        total = jnp.where(distance == k, c, jnp.where(distance == -k, -c, total))
    return total.astype(BF16)


NEAREST, SPARE = (3, 0), (0, 3)


def packed(rows, s):
    high, low = split(rows)
    moved = pltpu.roll(low.astype(F32), (SPARE[s] - NEAREST[s]) % rows.shape[0], 0)
    slot = iota(rows.shape, 0) % 4
    return jnp.where(slot == SPARE[s], moved, high.astype(F32)).astype(BF16)


def unpacked(rows, s):
    rows = rows.astype(F32)
    low = pltpu.roll(rows, (NEAREST[s] - SPARE[s]) % rows.shape[0], 0)
    return rows + jnp.where(iota(rows.shape, 0) % 4 == NEAREST[s], low, 0.0)


def skewed(rows, start, step):
    turn = iota(rows.shape, 0) % 4
    total = pltpu.roll(rows, start % 128, 1) if start % 128 else rows
    for n in range(1, 4):
        total = jnp.where(turn == n, pltpu.roll(rows, (start + step * n) % 128, 1), total)
    return total


def body_kernel(
    vel_in, lift_w_in, lift_b_in, conv_w_in, conv_b_in, head_w_in,
    out, stress_out,
    vel, lift_w, lift_b, conv_w, conv_b, head_w,
    xs, bx, ystage, ydec, ysend, csend, zvsend, yvsend, yvstage, wall,
    yland, cland, cpack, cfar, cwide, xland, zvland, yvland, xv, stx, sland,
    hid, taps, early, headk, strs, field, edge, base, e2, zd,
    send_sem, recv_sem, load_sem, ready, wrapped,
):
    here = (lax.axis_index("row"), lax.axis_index("col"), lax.axis_index("chan"))
    me = here[2]

    def peer(off):
        return tuple(
            h if o == 0 else lax.rem(h + (o + n) % n, n)
            for h, o, n in zip(here, off, (NROW, NCOL, NCHAN))
        )

    odd = lax.rem(here[0], 2)
    leftmost, rightmost = here[1] == 0, here[1] == NCOL - 1
    barrier = pltpu.get_barrier_semaphore()
    for off in NEAR:
        if off[1] < 1:
            pl.semaphore_signal(barrier, inc=1, device_id=peer(off), device_id_type=MESH)

    @pl.when(jnp.logical_not(rightmost))
    def _():
        for off in BEYOND:
            pl.semaphore_signal(barrier, inc=1, device_id=peer(off), device_id_type=MESH)

    @pl.when(odd == 0)
    def _():
        for off in FAR:
            pl.semaphore_signal(barrier, inc=1, device_id=peer(off), device_id_type=MESH)


    pairs_in = tuple((vel_in.at[n], vel.at[n]) for n in range(4)) + (
        (conv_w_in, conv_w), (lift_w_in, lift_w), (lift_b_in, lift_b),
        (conv_b_in, conv_b), (head_w_in, head_w),
    )
    loads = [
        pltpu.make_async_copy(src, dst, load_sem.at[k]) for k, (src, dst) in enumerate(pairs_in)
    ]
    for load in loads:
        load.start()
    copies = []

    def send(src, dst, source, landed=None, start=True):
        k = len(copies)
        copy = pltpu.make_async_remote_copy(
            src_ref=src, dst_ref=dst, send_sem=send_sem.at[k], recv_sem=recv_sem.at[k],
            device_id=peer(tuple(-s for s in source)), device_id_type=MESH,
        )
        if start:
            copy.start()
        if landed is not None:
            copies.append((copy, pltpu.make_async_remote_copy(
                src_ref=src, dst_ref=landed, send_sem=send_sem.at[k], recv_sem=recv_sem.at[k],
                device_id=peer(tuple(-s for s in source)), device_id_type=MESH,
            )))
        else:
            copies.append((copy, copy))
        return k

    def arrive(ks):
        for k in ks:
            copies[k][1].wait_recv()

    pool = jnp.where(iota((256, 128), 0) // 2 == iota((256, 128), 1), 1.0, 0.0).astype(BF16)
    r16 = iota((16, 256), 0)
    ends = jnp.where(r16 < 4, r16, r16 + 120)
    picker = jnp.where((iota((16, 256), 1) // 2 == ends) & (r16 < 8), 1.0, 0.0).astype(BF16)
    csend[...] = jnp.zeros_like(csend)
    ystage[...] = jnp.zeros_like(ystage)
    for p in range(2):
        loads[2 * p].wait()
        loads[2 * p + 1].wait()
        for c in range(3):
            both = vel[2 * p, c] + vel[2 * p + 1, c]
            r = 16 * (3 * p + c)
            xs[0, r : r + 16, :] = both[:, :128]
            xs[1, r : r + 16, :] = both[:, 128:]
    pairs = jnp.concatenate(
        [xs[h, pl.ds(0, 48, 2), :] + xs[h, pl.ds(1, 48, 2), :] for h in range(2)], axis=1
    )
    pieces = split3(pairs * 0.125)
    pooled = mm(jnp.concatenate(pieces, 0), pool)
    box = pooled[0:48] + pooled[48:96] + pooled[96:144]
    bx[0] = box[0:24]
    bx[1] = box[24:48]
    for p in range(2):
        for c in range(3):
            r = 8 * (3 * p + c)
            ystage[0, 16 * p + 4 * c : 16 * p + 4 * c + 4, :] = box[r + 4 : r + 8]
            ystage[1, 16 * p + 4 * c : 16 * p + 4 * c + 4, :] = box[r : r + 4]
    for s in range(2):
        ysend[s] = packed(ystage[s], s).reshape(2, 16, 128)
    columns = mm(picker, pieces[0], NT) + mm(picker, pieces[1], NT) + mm(picker, pieces[2], NT)
    csend[0, :, 0:48] = columns[4:8]
    csend[1, :, 0:48] = columns[0:4]
    ends8 = csend[...].reshape(8, 128)
    lane8 = iota((8, 128), 1)
    for p in range(2):
        mine = jnp.where((lane8 >= 24 * p) & (lane8 < 24 * p + 24), ends8, 0.0)
        spaced = skewed(mine, 128 - 24 * p, 32)
        for t in range(2):
            row = spaced[4 * t : 4 * t + 1]
            for n in range(1, 4):
                row = row + spaced[4 * t + n : 4 * t + n + 1]
            cpack[t, p] = row

    pl.semaphore_wait(
        barrier, len(NEAR) - jnp.where(leftmost, len(BEYOND), 0) + len(FAR) * odd
    )

    @pl.when(rightmost)
    def _():
        for off in BEYOND:
            pl.semaphore_signal(wrapped, inc=1, device_id=peer(off), device_id_type=MESH)

    ybox, corner, ycols, yvel = [], [], [], []
    for s, dr in ((0, -1), (1, 1)):
        ybox.append(send(ysend.at[s], yland.at[s, 1:3], (dr, 0, 0), start=False))
        ybox.append(send(ysend.at[s, 1], yland.at[s, 0], (dr, 0, -1), start=False))
        ybox.append(send(ysend.at[s, 0], yland.at[s, 3], (dr, 0, 1), start=False))
    for s, dr in ((0, -1), (1, 1)):
        for t, dc in ((0, -1), (1, 1)):
            corner += [
                send(cpack.at[t, 1], cfar.at[s, t, 0], (dr, dc, -1), start=False),
                send(cpack.at[t], cfar.at[s, t, 1:3], (dr, dc, 0), start=False),
                send(cpack.at[t, 0], cfar.at[s, t, 3], (dr, dc, 1), start=False),
            ]
    for s, dr in ((0, -1), (1, 1)):
        yvel.append(send(yvsend.at[s], yvland.at[s], (dr, 0, 0), start=False))
    far_copies = [copies[k][0] for k in ybox + corner]
    late_copies = [copies[k][0] for k in yvel]

    @pl.when(odd == 1)
    def _():
        for off in FAR:
            pl.semaphore_signal(ready, inc=1, device_id=peer(off), device_id_type=MESH)
        for copy in far_copies:
            copy.start()

    for t, dc in ((0, -1), (1, 1)):
        for dx in (-1, 0, 1):
            ycols.append(
                send(csend.at[t], cland.at[t, dx + 1], (0, dc, dx), start=dc == -1)
            )
    left_copies = [copies[k][0] for k in ycols[3:]]

    @pl.when(jnp.logical_not(leftmost))
    def _():
        for copy in left_copies:
            copy.start()

    xbox = [send(bx.at[1], xland.at[0], (0, 0, -1)), send(bx.at[0], xland.at[1], (0, 0, 1))]

    for k in range(12):
        yvstage[0, 4 * k : 4 * k + 4, :] = vel[k // 3, k % 3, 12:16, :]
        yvstage[1, 4 * k : 4 * k + 4, :] = vel[k // 3, k % 3, 0:4, :]
    for s in range(2):
        yvsend[s] = packed(yvstage[s], s)
    cwide[...] = jnp.zeros_like(cwide)

    for load in loads[4:]:
        load.wait()
    for k in range(9):
        a, c = k // 3, k % 3
        parts = [conv_w[9 * a + 3 * b + c].astype(F32) for b in range(3)]
        wall[me, 8 * k : 8 * k + 8, :] = jnp.concatenate(parts + [jnp.zeros((8, 32), F32)], axis=1)
    wall[me, 72:80, :] = jnp.zeros((8, 128), F32)
    wall[me, 72:78, 0:8] = head_w[...].astype(F32)
    wall[me, 78:79, 0:8] = conv_b[...].astype(F32)
    weights = [
        send(wall.at[me], wall.at[me], (0, 0, dx), wall.at[lax.rem(me + (dx + 4) % 4, 4)])
        for dx in (-1, 1, 2)
    ]
    rz = iota((16, 256), 0)
    at = jnp.where(rz < 8, rz + 248, rz - 8)
    take = jnp.where(iota((16, 256), 1) == at, 1.0, 0.0)
    zvsend[...] = jnp.zeros_like(zvsend)
    for c in range(3):
        cols = mm(take, vel[:, c].reshape(64, 256), NT, exact=True)
        zvsend[0, c, :, 0:64] = cols[0:8]
        zvsend[1, c, :, 0:64] = cols[8:16]
    zvel = [
        send(zvsend.at[t], zvland.at[t], (0, dc, 0), start=dc == -1) for t, dc in ((0, -1), (1, 1))
    ]

    @pl.when(jnp.logical_not(leftmost))
    def _():
        copies[zvel[1]][0].start()

    xvel = [send(vel.at[1:4], xv.at[0], (0, 0, -1)), send(vel.at[0:3], xv.at[1], (0, 0, 1))]

    spread = jnp.where(iota((32, 256), 1) % 32 == iota((32, 256), 0), 1.0, 0.0)
    bias = mm(lift_b[...], spread, exact=True)
    rows24 = jnp.where(iota((24, 3), 0) // 8 == iota((24, 3), 1), 1.0, 0.0)
    lift = mm(rows24, mm(lift_w[...], spread, exact=True), exact=True)
    lift = jnp.where(iota((24, 256), 0) % 8 == iota((24, 256), 1) // 32, lift, 0.0)
    lift_of = [
        jnp.concatenate([lift, jnp.zeros((104, 256), F32)], 0),
        jnp.concatenate([jnp.zeros((24, 256), F32), lift, jnp.zeros((80, 256), F32)], 0),
    ]

    def hold(q, row, lane, value):
        high, low = split(value)
        n, m = value.shape
        hid[q, row : row + n, lane : lane + m] = high
        hid[q, ZROWS + row : ZROWS + row + n, lane : lane + m] = low

    def lifted(rows):
        return jnp.tanh(mm(rows, lift, TN, exact=True) + bias)

    def side(dx):
        return jnp.concatenate(
            [cland[1, dx + 1], jnp.zeros((8, 128), F32), cland[0, dx + 1]], 0
        )

    PLANES = ((0, -1, 1), (1, 0, 0), (2, 0, 1), (3, 1, 0))
    for p in range(2):
        hold(p + 1, 0, 128, lifted(bx[p]))
    arrive(xbox)
    hold(0, 0, 128, lifted(xland[0]))
    hold(3, 0, 128, lifted(xland[1]))

    arrive(weights)
    lane = iota((32, 128), 1)
    zero = jnp.zeros((32, 128), F32)
    for k in range(9):
        a, c = k // 3, k % 3
        x = jnp.concatenate([wall[n, 8 * k : 8 * k + 8, :] for n in range(4)], 0)
        r1, r2, r3 = (pltpu.roll(x, 32 * n, 1) for n in (1, 2, 3))
        tiles = (
            (r1, zero),
            (jnp.where(lane >= 64, r2, 0.0), jnp.where(lane < 64, r2, 0.0)),
            (jnp.where(lane >= 96, r3, 0.0), jnp.where(lane < 96, r3, 0.0)),
            (zero, x),
        )
        for y, (first, second) in enumerate(tiles):
            r = 128 * c + 32 * y
            for h, half in enumerate((first, second)):
                taps[h, a, r : r + 32, 0:128] = half.astype(BF16)
                taps[h, a, r : r + 32, 128:256] = half.astype(BF16)

    @pl.when(odd == 1)
    def _():
        for copy in late_copies:
            copy.start()

    params = wall[0, 72:80, :]
    for n in range(1, 4):
        params = params + pltpu.roll(wall[n, 72:80, :], 8 * n, 1)
    rolled = [params] + [pltpu.roll(params, 32 * n, 1) for n in (1, 2, 3)]
    conv_bias = (rolled[0] + rolled[1] + rolled[2] + rolled[3])[6:7]
    for n in range(4):
        headk[pl.ds(n, 8, 4), :] = rolled[n]
    head = headk[...].astype(BF16)

    @pl.when(leftmost)
    def _():
        pl.semaphore_wait(wrapped, len(BEYOND))
        for copy in left_copies + [copies[zvel[1]][0]]:
            copy.start()

    arrive(ycols)
    for q, dx, p in PLANES:
        hold(q, 128, 128, jnp.tanh(mm(side(dx), lift_of[p], exact=True) + bias))

    def partial(h, tile):
        total = None
        for a in range(3):
            block = [hid[a : a + 2, n : n + ZROWS, 128 * tile : 128 * tile + 128] for n in (0, ZROWS)]
            block = jnp.concatenate(block, axis=2).reshape(2 * ZROWS, 256)
            term = mm(block, taps[h, a], NT)
            total = term if total is None else total + term
        return total

    def closure(g, total):
        for p in range(2):
            both = total[ZROWS * p : ZROWS * p + ZROWS]
            conv = (
                pltpu.roll(both[:, 0:128], 1, 0)
                + both[:, 128:256]
                + pltpu.roll(both[:, 256:384], ZROWS - 1, 0)
                + conv_bias
            )
            act = 0.5 * conv * (1.0 + jnp.tanh(0.5 * conv))
            high, low = split(act)
            found = mm(head, high, NT) + mm(head, low, NT)
            for s in range(6):
                strs[p, s, 4 * g : 4 * g + 4, 0:ZROWS] = found[4 * s : 4 * s + 4]

    closure(1, partial(0, 1) + partial(1, 2))
    early[0] = partial(1, 1)
    early[1] = partial(0, 2)

    field[...] = jnp.zeros_like(field)
    for p in range(4):
        uy = vel[p, 1]
        for i in range(3):
            field[p, i, 8:24, :] = uy * vel[p, i]
    stencil = stencil_matrix(iota((256, 256), 0) - iota((256, 256), 1))
    for i in range(3):
        flux = (vel[:, 2] * vel[:, i]).reshape(64, 256)
        base[:, i] = mm2(flux, stencil).reshape(4, 16, 256)
    for p in range(4):
        for i in range(3):
            total = base[p, i]
            for k, c in COEFS:
                total = total + c * (field[p, i, 8 + k : 24 + k, :] - field[p, i, 8 - k : 24 - k, :])
            base[p, i] = total
    arrive(zvel)
    r16z = iota((16, 256), 0)
    place = jnp.where(r16z < 8, r16z - 8, r16z + 248)
    rim = stencil_matrix(place - iota((16, 256), 1)).astype(F32)
    cols = [jnp.concatenate([zvland[0, c], zvland[1, c]], 0)[:, 0:64] for c in range(3)]
    for i in range(3):
        base[:, i] += mm(cols[2] * cols[i], rim, TN, exact=True).reshape(4, 16, 256)
    arrive(xvel)
    for i in range(3):
        planes = (
            [xv[0, n, 0] * xv[0, n, i] for n in range(3)]
            + [vel[n, 0] * vel[n, i] for n in range(4)]
            + [xv[1, n, 0] * xv[1, n, i] for n in range(3)]
        )
        for p in range(4):
            total = base[p, i]
            for k, c in COEFS:
                total = total + c * (planes[p + 3 + k] - planes[p + 3 - k])
            base[p, i] = total

    @pl.when(odd == 0)
    def _():
        pl.semaphore_wait(ready, len(FAR))
        for copy in far_copies:
            copy.start()

    arrive(ybox)

    @pl.when(odd == 0)
    def _():
        for copy in late_copies:
            copy.start()

    for s in range(2):
        ydec[s] = unpacked(yland[s].reshape(64, 128), s)
    for q in range(4):
        rows = jnp.concatenate(
            [ydec[s, 16 * q + 4 * c : 16 * q + 4 * c + 4, :] for c in range(3) for s in (1, 0)], 0
        )
        h = lifted(rows)
        hold(q, 0, 0, h[:, 128:256])
        hold(q, 0, 384, h[:, 0:128])
    arrive(corner)
    for q in range(4):
        for s in range(2):
            r = 16 * (2 * q + s)
            cwide[r : r + 4, :] = jnp.broadcast_to(cfar[s, 1, q], (4, 128))
            cwide[r + 12 : r + 16, :] = jnp.broadcast_to(cfar[s, 0, q], (4, 128))
    rows = skewed(cwide[...], 128, 96)
    h = jnp.tanh(mm(rows, lift_of[0], exact=True) + bias)
    for q in range(4):
        hold(q, 128, 0, h[32 * q : 32 * q + 16, 128:256])
        hold(q, 128, 384, h[32 * q + 16 : 32 * q + 32, 0:128])
    closure(0, early[0] + partial(0, 0))
    closure(2, early[1] + partial(1, 3))

    for p in range(2):
        for i, s in enumerate(X_COMPS):
            stx[p, i] = strs[p, s, 2:10, 0:128]
    xstress = [send(stx, sland.at[0], (0, 0, -1)), send(stx, sland.at[1], (0, 0, 1))]

    for p in range(2):
        for s in range(6):
            stress_out[p, s] = strs[p, s, 2:10, 0:128]

    arrive(yvel)
    edge[...] = jnp.zeros_like(edge)
    above, below = (unpacked(yvland[s], s) for s in range(2))
    for p in range(4):
        for i in range(3):
            k, y, n = 4 * (3 * p + i), 4 * (3 * p + 1), 3 * p + i
            edge[n, 4:8, :] = above[y : y + 4] * above[k : k + 4]
            edge[n, 16:20, :] = below[y : y + 4] * below[k : k + 4]
    for p in range(4):
        for i in range(3):
            n = 3 * p + i
            top = base[p, i, 0:8]
            bottom = base[p, i, 8:16]
            for k, c in COEFS:
                top = top - c * edge[n, 8 - k : 16 - k, :]
                bottom = bottom + c * edge[n, 8 + k : 16 + k, :]
            base[p, i, 0:8] = top
            base[p, i, 8:16] = bottom

    l144, c256 = iota((ZROWS, 256), 0), iota((ZROWS, 256), 1)
    dist = jnp.where(l144 < 136, l144, l144 - ZROWS) - c256 // 2
    even = jnp.where(dist == 0, 45.0, jnp.where(dist == -1, -36.0, jnp.where(dist == 1, -8.0, jnp.where(dist == -2, -1.0, 0.0))))
    odd = jnp.where(dist == 1, 36.0, jnp.where(dist == 0, -45.0, jnp.where(dist == -1, 8.0, jnp.where(dist == 2, 1.0, 0.0))))
    along = jnp.where(c256 % 2 == 0, even, odd).astype(BF16)
    zrows = jnp.concatenate(
        [strs[p, s, 2:10, 0:ZROWS] for p in range(2) for s in Z_COMPS], 0
    )
    zder = mm2(zrows, along)
    for p in range(2):
        for i in range(3):
            r = 8 * (3 * p + i)
            for half in range(2):
                piece = zder[r : r + 8, 128 * half : 128 * half + 128]
                zd[p, i, half, pl.ds(0, 8, 2), :] = piece
                zd[p, i, half, pl.ds(1, 8, 2), :] = piece
    yder = []
    for p in range(2):
        for i, s in enumerate(Y_COMPS):
            c = {k: strs[p, s, 2 + k : 10 + k, 0:128] for k in range(-2, 3)}
            yder.append((
                45.0 * c[0] - 36.0 * c[-1] - 8.0 * c[1] - c[-2],
                36.0 * c[1] - 45.0 * c[0] + 8.0 * c[-1] + c[2],
            ))
    double = jnp.where(iota((128, 256), 1) // 2 == iota((128, 256), 0), 1.0, 0.0).astype(BF16)

    arrive(xstress)
    for i in range(3):
        c = [sland[0, 0, i], sland[0, 1, i], stx[0, i], stx[1, i], sland[1, 0, i], sland[1, 1, i]]
        for p in range(2):
            n = p + 2
            xder = (
                45.0 * c[n] - 36.0 * c[n - 1] - 8.0 * c[n + 1] - c[n - 2],
                36.0 * c[n + 1] - 45.0 * c[n] + 8.0 * c[n - 1] + c[n + 2],
            )
            for px in range(2):
                for py in range(2):
                    e2[2 * p + px, i, pl.ds(py, 8, 2), :] = xder[px] + yder[3 * p + i][py]
    fine = mm2(e2[...].reshape(192, 128), double)
    for p in range(4):
        for i in range(3):
            r = 16 * (3 * p + i)
            zpart = jnp.concatenate([zd[p // 2, i, 0], zd[p // 2, i, 1]], axis=1)
            total = base[p, i] + fine[r : r + 16] + zpart
            out[p, i] = vel[p, i] - (0.1 / 60.0) * total

    for copy, _ in copies:
        copy.wait_send()


def body(velocity, lift_weight, lift_bias, conv_weight, conv_bias, head_weight):
    vmem = pl.BlockSpec(memory_space=pltpu.VMEM)
    ncopies = 6 + 12 + 6 + 2 + 2 + 3 + 2 + 2 + 2
    scratch = [
        pltpu.VMEM((4, 3, 16, 256), F32),
        pltpu.VMEM((3, 32), F32),
        pltpu.VMEM((1, 32), F32),
        pltpu.VMEM((27, 8, 32), BF16),
        pltpu.VMEM((1, 8), BF16),
        pltpu.VMEM((6, 8), BF16),
        pltpu.VMEM((2, 96, 128), F32),
        pltpu.VMEM((2, 24, 128), F32),
        pltpu.VMEM((2, 32, 128), F32),
        pltpu.VMEM((2, 64, 128), F32),
        pltpu.VMEM((2, 2, 16, 128), BF16),
        pltpu.VMEM((2, 4, 128), F32),
        pltpu.VMEM((2, 3, 8, 128), F32),
        pltpu.VMEM((2, 48, 256), BF16),
        pltpu.VMEM((2, 48, 256), F32),
        pltpu.VMEM((4, 80, 128), F32),
        pltpu.VMEM((2, 4, 16, 128), BF16),
        pltpu.VMEM((2, 3, 4, 128), F32),
        pltpu.VMEM((2, 2, 1, 128), F32),
        pltpu.VMEM((2, 2, 4, 1, 128), F32),
        pltpu.VMEM((128, 128), F32),
        pltpu.VMEM((2, 24, 128), F32),
        pltpu.VMEM((2, 3, 8, 128), F32),
        pltpu.VMEM((2, 48, 256), BF16),
        pltpu.VMEM((2, 3, 3, 16, 256), F32),
        pltpu.VMEM((2, 3, 8, 128), F32),
        pltpu.VMEM((2, 2, 3, 8, 128), F32),
        pltpu.VMEM((4, 2 * ZROWS, 512), BF16),
        pltpu.VMEM((2, 3, 384, 256), BF16),
        pltpu.VMEM((2, 2 * ZROWS, 384), F32),
        pltpu.VMEM((32, 128), F32),
        pltpu.VMEM((2, 6, 16, 256), F32),
        pltpu.VMEM((4, 3, 32, 256), F32),
        pltpu.VMEM((12, 24, 256), F32),
        pltpu.VMEM((4, 3, 16, 256), F32),
        pltpu.VMEM((4, 3, 16, 128), F32),
        pltpu.VMEM((2, 3, 2, 16, 128), F32),
        pltpu.SemaphoreType.DMA((ncopies,)),
        pltpu.SemaphoreType.DMA((ncopies,)),
        pltpu.SemaphoreType.DMA((9,)),
        pltpu.SemaphoreType.REGULAR,
        pltpu.SemaphoreType.REGULAR,
    ]
    return pl.pallas_call(
        body_kernel,
        out_shape=(
            pltpu.VMEM((4, 3, 16, 256), F32),
            pltpu.VMEM((2, 6, 8, 128), F32),
        ),
        in_specs=[pl.BlockSpec(memory_space=pltpu.HBM)] * 6,
        out_specs=(vmem, vmem),
        scratch_shapes=scratch,
        compiler_params=pltpu.CompilerParams(
            collective_id=0, has_side_effects=True, vmem_limit_bytes=60 * 2**20
        ),
    )(
        velocity,
        lift_weight.T,
        lift_bias.reshape(1, 32),
        conv_weight,
        conv_bias.reshape(1, 8),
        head_weight,
    )


def solution(mesh):
    placed = (
        P("chan", None, "row", "col"),
        P(),
        P(),
        P(None, "chan", None),
        P("chan"),
        P(None, "chan"),
    )
    return jax.shard_map(
        body,
        mesh=mesh,
        in_specs=placed,
        out_specs=(P("chan", None, "row", "col"), P("chan", None, "row", "col")),
        check_vma=False,
    )
```
